128 devices in a mesh: grid: 32 (over y, x, core), band: 4 (over z).
Axes of the slice: x: 4, y: 4, z: 4, core: 2. Of those that a mesh axis runs over, the one named last changes fastest.
Arguments:
- residual: float32 [32, 256, 32, 384], P('band', 'grid')
- direction: float32 [32, 256, 32, 384], P('band', 'grid'), may hold values from -2 to 2
- solution: float32 [32, 256, 32, 384], P('band', 'grid'), may hold values from -6 to 6
- old_product: float32 [32], P('band'), may hold values from 629145.6 to 2516582.5
- orbitals: bfloat16 [32, 256, 32, 384], P('band', 'grid')
- energies: float32 [32], replicated, may hold values from -3 to -0.3
- potential: float32 [256, 32, 384], P('grid'), may hold values from 0.5 to 3
- column_index: int32 [32], P('band'), may hold values from 0 to 95
- panel_index: int32 [32], P('band'), may hold values from 0 to 1
Outputs:
- new_solution: float32 [32, 256, 32, 384], P('band', 'grid')
- new_residual: float32 [32, 256, 32, 384], P('band', 'grid')
- new_direction: float32 [32, 256, 32, 384], P('band', 'grid')
- new_product: float32 [32], P('band')
The draws below stay inside these ranges and needn't reach their ends.
All inputs are finite; a program needn't handle non-finite values.
Results may differ from the reference program's by a relative error of at most 0.00085.
Values may be sent and summed in bfloat16 or wider, within the bound.
A program may use at most 128 MiB of HBM per device.

```python
import math
import jax
import jax.numpy as jnp
from jax import lax

NY = 32
NZ = 384
PB = 16
PANELS = 2
NBANDS = 32
NCOLS = 96
C = 32
NX = 256


def shared_orbitals(key):
    return jax.random.normal(key, (NBANDS, NX, NY, NZ), jnp.float32)


def draw_orbitals(key, part):
    base = shared_orbitals(key)
    return base.astype(jnp.bfloat16)


def draw_residual(key, part):
    base = shared_orbitals(key)
    key = jax.random.fold_in(key, 23)
    weight_key, noise_key = jax.random.split(key)
    weights = 0.4 * jax.random.normal(weight_key, (C, NBANDS), jnp.float32)
    noise = jax.random.normal(noise_key, (C, NX, NY, NZ), jnp.float32)
    mixed = jnp.einsum('cb,bxyz->cxyz', weights, base, precision=lax.Precision.HIGHEST)
    return (noise + mixed).astype(jnp.float32)


def with_ends(array, rng, least, largest):
    dims = array.shape
    spot = [jax.random.randint(jax.random.fold_in(rng, axis), (), 0, dims[axis]) for axis in range(len(dims))]
    array = array.at[tuple(spot)].set(least)
    longest = dims.index(max(dims))
    spot[longest] = (spot[longest] + 1) % dims[longest]
    return array.at[tuple(spot)].set(largest)


def steps_of(key, extent, cuts, least, high):
    loudness, own = 1.0, jax.random.fold_in(key, 6)
    for dim, shards_of in cuts:
        draws = jnp.exp(jax.random.uniform(jax.random.fold_in(own, dim), (shards_of,), jnp.float32, least / len(cuts), high / len(cuts)))
        loudness = loudness * jnp.repeat(draws, extent[dim] // shards_of).reshape([-1 if axis == dim else 1 for axis in range(len(extent))])
    return loudness


def gaussian(stream_key, dims, width, limit, cuts=(), kind=jnp.bfloat16):
    result = width * jax.random.normal(stream_key, dims, jnp.float32)
    if cuts:
        result = result * steps_of(stream_key, dims, cuts, -0.22, 0.18)
    return jnp.clip(result, -limit, limit).astype(kind)


def setup_inputs(seed: int = 0) -> dict:
    splits = jax.random.split(jax.random.key(seed), 10)
    residual = draw_residual(jax.random.fold_in(splits[9], 71), 0)
    direction = gaussian(splits[1], (C, NX, NY, NZ), 0.3, 2.0, ((0, 4), (1, 32)), jnp.float32)
    solution = gaussian(splits[2], (C, NX, NY, NZ), 1.0, 6.0, ((0, 4), (1, 32)), jnp.float32)
    old_product = jnp.clip(jnp.exp(math.log(2516582.5) - 1.3862944 * jax.random.uniform(splits[3], (C,), jnp.float32) ** steps_of(splits[3], (C,), ((0, 4),), -0.2, 0.2)), 629145.6, 2516582.5)
    orbitals = draw_orbitals(jax.random.fold_in(splits[9], 71), 0)
    energies = jnp.clip(jax.random.uniform(splits[5], (NBANDS,), jnp.float32, -3.0, -0.3), -3.0, -0.3)
    potential = jnp.clip(0.5 + 2.5 * jax.random.uniform(splits[6], (NX, NY, NZ), jnp.float32) ** steps_of(splits[6], (NX, NY, NZ), ((0, 32),), -0.2, 0.2), 0.5, 3.0)
    column_index = with_ends(jax.random.randint(splits[7], (C,), 0, NCOLS), jax.random.fold_in(splits[7], 1), 0, NCOLS - 1).astype(jnp.int32)
    panel_index = with_ends(jax.random.randint(splits[8], (C,), 0, PANELS), jax.random.fold_in(splits[8], 1), 0, PANELS - 1).astype(jnp.int32)
    return {"residual": residual, "direction": direction, "solution": solution, "old_product": old_product, "orbitals": orbitals, "energies": energies, "potential": potential, "column_index": column_index, "panel_index": panel_index}


COEFFS = (-49.0 / 18.0, 3.0 / 2.0, -3.0 / 20.0, 1.0 / 90.0)


def operator_three(column, shifted):
    padded = jnp.pad(column, 3)
    extent_x, extent_y, extent_z = column.shape
    summed = 3.0 * COEFFS[0] * column
    for offset in range(1, 4):
        beside_all = padded[3 + offset:3 + offset + extent_x, 3:3 + extent_y, 3:3 + extent_z] + padded[3 - offset:3 - offset + extent_x, 3:3 + extent_y, 3:3 + extent_z]
        beside_all = beside_all + padded[3:3 + extent_x, 3 + offset:3 + offset + extent_y, 3:3 + extent_z] + padded[3:3 + extent_x, 3 - offset:3 - offset + extent_y, 3:3 + extent_z]
        beside_all = beside_all + padded[3:3 + extent_x, 3:3 + extent_y, 3 + offset:3 + offset + extent_z] + padded[3:3 + extent_x, 3:3 + extent_y, 3 - offset:3 - offset + extent_z]
        summed = summed + COEFFS[offset] * beside_all
    return -0.5 * summed + shifted * column


def reference(residual, direction, solution, old_product, orbitals, energies, potential, column_index, panel_index):
    wave = orbitals.astype(jnp.float32)
    cells = float(NX * NY * NZ)
    band_ids = jnp.arange(NBANDS, dtype=jnp.int32)

    def one_column(items):
        res_col, dir_col, sol_col, old_col, col_id, panel_id = items
        energy = jnp.sum(jnp.where(band_ids == col_id // 3, energies, jnp.float32(0.0)))
        shifted = potential - energy
        precond = shifted - 1.5 * COEFFS[0]
        start = res_col / precond
        correlation = jnp.einsum('xyz,bxyz->b', start, wave, precision=lax.Precision.HIGHEST)
        chosen = jnp.where(band_ids // PB == panel_id, correlation, jnp.float32(0.0)) / cells
        projected = start - jnp.einsum('b,bxyz->xyz', chosen, wave, precision=lax.Precision.HIGHEST)
        rr_now = jnp.sum(res_col * projected)
        new_dir = projected + (rr_now / old_col) * dir_col
        image = operator_three(new_dir, shifted)
        curvature = jnp.sum(new_dir * image)
        step_size = rr_now / curvature
        return sol_col + step_size * new_dir, res_col - step_size * image, new_dir, rr_now

    outputs = lax.map(one_column, (residual, direction, solution, old_product, column_index, panel_index))
    return (outputs[0], outputs[1], outputs[2], outputs[3])
```

```python
import functools

import jax
import jax.numpy as jnp
from jax import lax
from jax.experimental import pallas as pl
from jax.experimental.pallas import tpu as pltpu
from jax.sharding import PartitionSpec as P

MESH = pl.DeviceIdType.MESH
F32 = jnp.float32
BF16 = jnp.bfloat16

PB = 16
K0, K1, K2, K3 = (-49.0 / 18.0, 3.0 / 2.0, -3.0 / 20.0, 1.0 / 90.0)
SCALED = (135.0, -13.5, 1.0)
UNSCALE = -0.5 / 90.0

COLS = 8
BANDS = 8
XS = 8
NY = 32
NZ = 384
HALF = 16
HALO = 3
CHUNKS = 4


def iota(shape, dim):
    return lax.broadcasted_iota(jnp.int32, shape, dim)


def coefficient(distance):
    gap = jnp.abs(distance)
    return jnp.where(
        gap == 1, SCALED[0], jnp.where(gap == 2, SCALED[1], jnp.where(gap == 3, SCALED[2], 0.0))
    )


def dot(left, right, dims=((1,), (0,)), precision=None):
    return lax.dot_general(
        left, right, (dims, ((), ())), precision=precision, preferred_element_type=F32
    )


def first_kernel(
    groups,
    res_hbm,
    dir_hbm,
    orb_hbm,
    pot_hbm,
    old_ref,
    energy_ref,
    column_ref,
    panel_ref,
    new_dir,
    image,
    rr_out,
    step_out,
    start,
    direction,
    pot,
    wave,
    left,
    acc,
    kron,
    sten,
    sten_halo,
    sten_z,
    halo_out,
    halo_in,
    sums,
    curves,
    partial,
    local_sem,
    ring_send,
    ring_recv,
    sum_send,
    sum_recv,
    halo_send,
    halo_recv,
):
    g = lax.axis_index("grid")
    z = lax.axis_index("band")
    up, down = lax.rem(z + 1, 4), lax.rem(z + 3, 4)

    loads = [
        pltpu.make_async_copy(src, dst, local_sem.at[i])
        for i, (src, dst) in enumerate(
            ((res_hbm, start), (pot_hbm, pot), (orb_hbm, wave.at[0]), (dir_hbm, direction))
        )
    ]
    for load in loads:
        load.start()

    barrier = pltpu.get_barrier_semaphore()
    for to in (up, down):
        pl.semaphore_signal(barrier, inc=1, device_id=(g, to), device_id_type=MESH)

    def greet(k, _):
        pl.semaphore_signal(
            barrier, inc=1, device_id=(lax.rem(g + k, groups), z), device_id_type=MESH
        )
        return 0

    lax.fori_loop(1, groups, greet, 0)
    pl.semaphore_wait(barrier, groups + 1)

    def ring(src, dst, i, to):
        return pltpu.make_async_remote_copy(
            src_ref=src,
            dst_ref=dst,
            send_sem=ring_send.at[i],
            recv_sem=ring_recv.at[i],
            device_id=(g, to),
            device_id_type=MESH,
        )

    low, high = pl.ds(0, BANDS // 2), pl.ds(BANDS // 2, BANDS // 2)
    low_up = ring(orb_hbm.at[low], wave.at[1, low], 0, up)
    high_down = ring(orb_hbm.at[high], wave.at[3, high], 1, down)
    high_up = ring(orb_hbm.at[high], wave.at[1, high], 2, up)
    low_down = ring(orb_hbm.at[low], wave.at[3, low], 3, down)
    low_up.start()
    high_down.start()
    high_up.start()
    low_down.start()

    rows, cols = iota((256, 256), 0), iota((256, 256), 1)
    dx, dy = rows // NY - cols // NY, rows % NY - cols % NY
    sten[...] = jnp.where(
        dy == 0, coefficient(dx), jnp.where(dx == 0, coefficient(dy), 0.0)
    ).astype(BF16)
    rows, cols = iota((256, 192), 0), iota((256, 192), 1)
    plane = cols // NY
    there = jnp.where(plane < HALO, plane - HALO, plane - HALO + XS)
    inside = jnp.where(plane < HALO, g, groups - 1 - g) > 0
    sten_halo[...] = jnp.where(
        jnp.logical_and(inside, rows % NY == cols % NY), coefficient(rows // NY - there), 0.0
    ).astype(BF16)
    sten_z[...] = coefficient(iota((NZ, NZ), 0) - iota((NZ, NZ), 1)).astype(BF16)

    def shift_of(c):
        return energy_ref[column_ref[c] // 3]

    loads[0].wait()
    loads[1].wait()

    def start_column(c, _):
        e = shift_of(c)

        def start_plane(x, total):
            r = start[c, x]
            s = r / (pot[x] - e - 1.5 * K0)
            start[c, x] = s
            for h in range(2):
                part = slice(h * HALF, (h + 1) * HALF)
                left[x, h, 0, c] = s[part].astype(BF16)
                left[x, h, 1, c] = r[part].astype(BF16)
            return total + jnp.sum((r * s).reshape(4, 8, NZ), axis=0)

        total = lax.fori_loop(0, XS, start_plane, jnp.zeros((8, NZ), F32))
        partial[c] = total[:, :128] + total[:, 128:256] + total[:, 256:]
        return 0

    lax.fori_loop(0, COLS, start_column, 0)

    def correlate(slot, first, planes):
        def body(x, total):
            for h in range(2):
                total = total + dot(
                    left[x, h].reshape(256, NZ),
                    wave[slot, :, x, pl.ds(h * HALF, HALF), :].reshape(128, NZ),
                    ((1,), (1,)),
                )
            return total

        return lax.fori_loop(first, first + planes, body, jnp.zeros((256, 128), F32))

    loads[2].wait()
    acc[:, 0:128] = correlate(0, 0, XS)

    forwards = []
    low_up.wait_recv()
    for q in range(CHUNKS):
        part = pl.ds(q * XS // CHUNKS, XS // CHUNKS)
        copy = ring(wave.at[1, low, part], wave.at[2, low, part], 4 + 2 * q, up)
        copy.start()
        forwards.append(copy)
    high_down.wait_recv()
    for q in range(CHUNKS):
        part = pl.ds(q * XS // CHUNKS, XS // CHUNKS)
        copy = ring(wave.at[3, high, part], wave.at[2, high, part], 5 + 2 * q, down)
        copy.start()
        forwards.append(copy)
    high_up.wait_recv()
    acc[:, 128:256] = correlate(1, 0, XS)
    low_down.wait_recv()
    acc[:, 384:512] = correlate(3, 0, XS)
    for q in range(CHUNKS):
        forwards[q].wait_recv()
        forwards[CHUNKS + q].wait_recv()
        part = correlate(2, q * XS // CHUNKS, XS // CHUNKS)
        acc[:, 256:384] = part if q == 0 else acc[:, 256:384] + part

    same = iota((256, 512), 0) % HALF == iota((256, 512), 1) % HALF
    folded = jnp.sum(jnp.where(same, acc[...], 0.0).reshape(16, HALF, 512), axis=1)
    pick = iota((512, 128), 0) // HALF
    lane = iota((512, 128), 1)
    mine = dot(
        folded[:8], jnp.where(pick == lane, 1.0, 0.0), precision=lax.Precision.HIGHEST
    ) + dot(
        folded[8:], jnp.where(pick + 32 == lane, 1.0, 0.0), precision=lax.Precision.HIGHEST
    )
    lane = iota((8, 128), 1)
    own = jnp.sum(jnp.sum(partial[...], axis=1), axis=1, keepdims=True)
    mine = mine + jnp.where(lane == 64, own, 0.0)

    def add_over_grid(table, value, k):
        table[g] = value

        def send(i, _):
            pltpu.make_async_remote_copy(
                src_ref=table.at[g],
                dst_ref=table.at[g],
                send_sem=sum_send.at[k],
                recv_sem=sum_recv.at[k],
                device_id=(lax.rem(g + i, groups), z),
                device_id_type=MESH,
            ).start()
            return 0

        lax.fori_loop(1, groups, send, 0)
        others = table.at[pl.ds(0, groups - 1)]
        pltpu.make_async_copy(others, others, sum_recv.at[k]).wait()
        total = jnp.sum(table[...], axis=0)
        pltpu.make_async_copy(others, others, sum_send.at[k]).wait()
        return total

    total = add_over_grid(sums, mine, 0)

    owner = lax.rem(z + jnp.where(lane < 8, 0, jnp.where(lane < 16, 3, jnp.where(lane < 24, 2, 1))), 4)
    column = iota((8, 128), 0)
    panel = jnp.zeros((8, 128), jnp.int32)
    old = jnp.zeros((8, 128), F32)
    for c in range(COLS):
        panel = jnp.where(column == c, panel_ref[c], panel)
        old = jnp.where(column == c, old_ref[c], old)
    cells = float(groups * XS * NY * NZ)
    chosen = jnp.where(
        jnp.logical_and(lane < 32, owner * BANDS // PB == panel), total, 0.0
    ) / cells
    overlap = pltpu.roll(total, 96, 1)
    rr = jnp.sum(
        jnp.where(lane == 64, total, 0.0) - chosen * overlap, axis=1, keepdims=True
    )
    rr = jnp.broadcast_to(rr, (8, 128))
    rr_out[...] = rr
    beta = rr / old

    top = chosen.astype(BF16)
    rest = (chosen - top.astype(F32)).astype(BF16)
    pair = jnp.concatenate([top.astype(F32), rest.astype(F32)], axis=0).astype(BF16)
    spread = dot(
        jnp.where(iota((256, 16), 0) // HALF == iota((256, 16), 1), 1.0, 0.0).astype(BF16), pair
    ).astype(BF16)
    spread = dot(
        spread,
        jnp.where(iota((128, 512), 1) // HALF == iota((128, 512), 0), 1.0, 0.0).astype(BF16),
    )
    kron[...] = jnp.where(same, spread, 0.0).astype(BF16)

    loads[3].wait()

    def project(x, face, k):
        for h in range(2):
            part = pl.ds(h * HALF, HALF)
            removed = dot(kron[...], wave[:, :, x, part, :].reshape(512, NZ))
            for c in range(COLS):
                gone = removed[c * HALF : (c + 1) * HALF] + removed[128 + c * HALF : 128 + (c + 1) * HALF]
                value = start[c, x, part] - gone + beta[c : c + 1, :1] * direction[c, x, part]
                new_dir[c, x, part] = value
                if face is not None:
                    halo_out[face, c, k, part] = value.astype(BF16)

    def halo(face, to):
        return pltpu.make_async_remote_copy(
            src_ref=halo_out.at[face],
            dst_ref=halo_in.at[1 - face],
            send_sem=halo_send.at[face],
            recv_sem=halo_recv.at[face],
            device_id=(to, z),
            device_id_type=MESH,
        )

    to_left = halo(0, lax.rem(g + groups - 1, groups))
    to_right = halo(1, lax.rem(g + 1, groups))

    def face_plane(face, x, k):
        project(x, face, k)
        return 0

    lax.fori_loop(0, HALO, lambda k, _: face_plane(0, k, k), 0)
    to_left.start()
    lax.fori_loop(0, HALO, lambda k, _: face_plane(1, XS - HALO + k, k), 0)
    to_right.start()
    lax.fori_loop(HALO, XS - HALO, lambda x, _: face_plane(None, x, None), 0)

    def inner(c, _):
        value = new_dir[c].reshape(256, NZ)
        top = value.astype(BF16)
        rest = (value - top.astype(F32)).astype(BF16)
        beside = dot(sten[...], top) + dot(sten[...], rest)
        beside = beside + (dot(top, sten_z[...]) + dot(rest, sten_z[...]))
        local = pot[...].reshape(256, NZ) - shift_of(c) - 1.5 * K0
        image[c] = (UNSCALE * beside + local * value).reshape(XS, NY, NZ)
        return 0

    lax.fori_loop(0, COLS, inner, 0)
    to_left.wait_recv()
    to_right.wait_recv()

    def outer(c, _):
        beside = dot(sten_halo[:, 0:96], halo_in[0, c].reshape(96, NZ)) + dot(
            sten_halo[:, 96:192], halo_in[1, c].reshape(96, NZ)
        )
        full = image[c].reshape(256, NZ) + UNSCALE * beside
        image[c] = full.reshape(XS, NY, NZ)
        total = jnp.sum((full * new_dir[c].reshape(256, NZ)).reshape(32, 8, NZ), axis=0)
        partial[c] = total[:, :128] + total[:, 128:256] + total[:, 256:]
        return 0

    lax.fori_loop(0, COLS, outer, 0)
    curvature = jnp.sum(add_over_grid(curves, jnp.sum(partial[...], axis=1), 1), axis=1, keepdims=True)
    step_out[...] = rr / curvature

    to_left.wait_send()
    to_right.wait_send()
    for copy in (low_up, high_down, high_up, low_down, *forwards):
        copy.wait_send()


def last_kernel(step, solution_in, residual_in, new_dir, image, solution_out, residual_out, dir_out):
    c = pl.program_id(0)
    alpha = step[pl.ds(c, 1), :1]
    p = new_dir[0]
    solution_out[0] = solution_in[0] + alpha * p
    residual_out[0] = residual_in[0] - alpha * image[0]
    dir_out[0] = p


def on_device(groups, residual, direction, solution, old_product, orbitals, energies, potential, column_index, panel_index):
    field = (COLS, XS, NY, NZ)
    any_spec = pl.BlockSpec(memory_space=pl.ANY)
    smem = pl.BlockSpec(memory_space=pltpu.SMEM)
    vmem = pl.BlockSpec(memory_space=pltpu.VMEM)
    dma = pltpu.SemaphoreType.DMA
    new_dir, image, rr, step = pl.pallas_call(
        functools.partial(first_kernel, groups),
        out_shape=(
            jax.ShapeDtypeStruct(field, F32),
            jax.ShapeDtypeStruct(field, F32),
            jax.ShapeDtypeStruct((8, 128), F32),
            jax.ShapeDtypeStruct((8, 128), F32),
        ),
        in_specs=[any_spec] * 4 + [smem] * 4,
        out_specs=(vmem, vmem, vmem, vmem),
        scratch_shapes=[
            pltpu.VMEM(field, F32),
            pltpu.VMEM(field, F32),
            pltpu.VMEM((XS, NY, NZ), F32),
            pltpu.VMEM((4, BANDS, XS, NY, NZ), BF16),
            pltpu.VMEM((XS, 2, 2, COLS, HALF, NZ), BF16),
            pltpu.VMEM((256, 512), F32),
            pltpu.VMEM((256, 512), BF16),
            pltpu.VMEM((256, 256), BF16),
            pltpu.VMEM((256, 192), BF16),
            pltpu.VMEM((NZ, NZ), BF16),
            pltpu.VMEM((2, COLS, HALO, NY, NZ), BF16),
            pltpu.VMEM((2, COLS, HALO, NY, NZ), BF16),
            pltpu.VMEM((groups, 8, 128), F32),
            pltpu.VMEM((groups, 8, 128), F32),
            pltpu.VMEM((COLS, 8, 128), F32),
            dma((4,)),
            dma((4 + 2 * CHUNKS,)),
            dma((4 + 2 * CHUNKS,)),
            dma((2,)),
            dma((2,)),
            dma((2,)),
            dma((2,)),
        ],
        compiler_params=pltpu.CompilerParams(
            collective_id=0, has_side_effects=True, vmem_limit_bytes=40 << 20
        ),
        name="project_and_apply",
    )(residual, direction, orbitals, potential, old_product, energies, column_index, panel_index)

    block = pl.BlockSpec((1, XS, NY, NZ), lambda c: (c, 0, 0, 0))
    new_solution, new_residual, out_dir = pl.pallas_call(
        last_kernel,
        grid=(COLS,),
        out_shape=tuple(jax.ShapeDtypeStruct(field, F32) for _ in range(3)),
        in_specs=[pl.BlockSpec((8, 128), lambda c: (0, 0)), block, block, block, block],
        out_specs=(block, block, block),
        compiler_params=pltpu.CompilerParams(vmem_limit_bytes=16 << 20),
        name="take_step",
    )(step, solution, residual, new_dir, image)
    return new_solution, new_residual, out_dir, rr[:, 0]


def solution(mesh):
    field = P("band", "grid", None, None)
    return jax.shard_map(
        functools.partial(on_device, mesh.shape["grid"]),
        mesh=mesh,
        in_specs=(
            field,
            field,
            field,
            P("band"),
            field,
            P(),
            P("grid", None, None),
            P("band"),
            P("band"),
        ),
        out_specs=(field, field, field, P("band")),
        check_vma=False,
    )
```

```python
import functools

import jax
import jax.numpy as jnp
from jax import lax
from jax.experimental import pallas as pl
from jax.experimental.pallas import tpu as pltpu
from jax.sharding import PartitionSpec as P

MESH = pl.DeviceIdType.MESH
F32 = jnp.float32
BF16 = jnp.bfloat16

PB = 16
K0, K1, K2, K3 = (-49.0 / 18.0, 3.0 / 2.0, -3.0 / 20.0, 1.0 / 90.0)
SCALED = (135.0, -13.5, 1.0)
UNSCALE = -0.5 / 90.0

COLS = 8
BANDS = 8
XS = 8
NY = 32
NZ = 384
HALF = 16
HALO = 3
PIECES = (pl.ds(0, HALO), pl.ds(XS - HALO, HALO), pl.ds(HALO, XS - 2 * HALO))
FACES = PIECES[:2]


def iota(shape, dim):
    return lax.broadcasted_iota(jnp.int32, shape, dim)


def coefficient(distance):
    gap = jnp.abs(distance)
    return jnp.where(
        gap == 1, SCALED[0], jnp.where(gap == 2, SCALED[1], jnp.where(gap == 3, SCALED[2], 0.0))
    )


def dot(left, right, dims=((1,), (0,)), precision=None):
    return lax.dot_general(
        left, right, (dims, ((), ())), precision=precision, preferred_element_type=F32
    )


def first_kernel(
    groups,
    res_hbm,
    dir_hbm,
    orb_hbm,
    pot_hbm,
    old_hbm,
    energy_hbm,
    column_hbm,
    panel_hbm,
    new_dir,
    image,
    rr_out,
    step_out,
    start,
    direction,
    pot,
    wave,
    left,
    acc,
    kron,
    sten,
    sten_z,
    halo_wave,
    halo_out,
    halo_start,
    halo_in,
    halo_dir,
    sums,
    curves,
    partial,
    old_ref,
    energy_ref,
    column_ref,
    panel_ref,
    local_sem,
    ring_send,
    ring_recv,
    sum_send,
    sum_recv,
    halo_send,
    halo_recv,
):
    g = lax.axis_index("grid")
    z = lax.axis_index("band")
    up, down = lax.rem(z + 1, 4), lax.rem(z + 3, 4)

    loads = [
        pltpu.make_async_copy(src, dst, local_sem.at[i])
        for i, (src, dst) in enumerate(
            (
                (column_hbm, column_ref),
                (energy_hbm, energy_ref),
                (pot_hbm, pot),
                (res_hbm, start),
                (orb_hbm, wave.at[0]),
                (dir_hbm, direction),
                (old_hbm, old_ref),
                (panel_hbm, panel_ref),
            )
        )
    ]
    for load in loads:
        load.start()

    barrier = pltpu.get_barrier_semaphore()
    for to in (up, down):
        pl.semaphore_signal(barrier, inc=1, device_id=(g, to), device_id_type=MESH)

    for k in range(1, groups):
        pl.semaphore_signal(
            barrier, inc=1, device_id=(lax.rem(g + k, groups), z), device_id_type=MESH
        )
    pl.semaphore_wait(barrier, groups + 1)

    def ring(src, dst, i, to):
        return pltpu.make_async_remote_copy(
            src_ref=src,
            dst_ref=dst,
            send_sem=ring_send.at[i],
            recv_sem=ring_recv.at[i],
            device_id=(g, to),
            device_id_type=MESH,
        )

    sides = (lax.rem(g + groups - 1, groups), lax.rem(g + 1, groups))

    def halo(src, dst, i, face):
        return pltpu.make_async_remote_copy(
            src_ref=src,
            dst_ref=dst,
            send_sem=halo_send.at[i],
            recv_sem=halo_recv.at[i],
            device_id=(sides[face], z),
            device_id_type=MESH,
        )

    landing = (pl.ds(HALO, HALO), pl.ds(0, HALO))
    halos = []

    def send_faces(slot, bands, src=None):
        src = wave.at[slot] if src is None else src
        for face in range(2):
            send_face(slot, bands, face, src)

    def send_face(slot, bands, face, src):
        copy = halo(
            src.at[bands, FACES[face]], halo_wave.at[slot, bands, landing[face]], len(halos), face
        )
        copy.start()
        halos.append(copy)

    low, high = pl.ds(0, BANDS // 2), pl.ds(BANDS // 2, BANDS // 2)
    low_up = ring(orb_hbm.at[low], wave.at[1, low], 0, up)
    high_down = ring(orb_hbm.at[high], wave.at[3, high], 1, down)
    high_up = ring(orb_hbm.at[high], wave.at[1, high], 2, up)
    low_down = ring(orb_hbm.at[low], wave.at[3, low], 3, down)
    low_up.start()
    high_down.start()
    high_up.start()
    low_down.start()
    send_faces(0, pl.ds(0, BANDS), orb_hbm)

    rows, cols = iota((256, 448), 0), iota((256, 448), 1)
    plane = cols // NY
    there = jnp.where(plane < XS, plane, jnp.where(plane < XS + HALO, plane - XS - HALO, plane - HALO))
    inside = jnp.where(plane < XS, 1, jnp.where(plane < XS + HALO, g, groups - 1 - g)) > 0
    dx, dy = rows // NY - there, rows % NY - cols % NY
    weight = jnp.where(dy == 0, coefficient(dx), jnp.where(dx == 0, coefficient(dy), 0.0))
    sten[...] = jnp.where(inside, weight, 0.0).astype(BF16)
    sten_z[...] = coefficient(iota((NZ, NZ), 0) - iota((NZ, NZ), 1)).astype(BF16)

    def shift_of(c):
        return energy_ref[column_ref[c] // 3]

    for load in loads[:4]:
        load.wait()

    def start_column(c, _):
        e = shift_of(c)

        def start_plane(x, total):
            r = start[c, x]
            s = r / (pot[x] - e - 1.5 * K0)
            start[c, x] = s
            for h in range(2):
                part = slice(h * HALF, (h + 1) * HALF)
                left[x, h, 0, c] = s[part].astype(BF16)
                left[x, h, 1, c] = r[part].astype(BF16)
            return total + jnp.sum((r * s).reshape(4, 8, NZ), axis=0)

        total = lax.fori_loop(0, XS, start_plane, jnp.zeros((8, NZ), F32))
        partial[c] = total[:, :128] + total[:, 128:256] + total[:, 256:]
        return 0

    lax.fori_loop(0, COLS, start_column, 0)
    for face in range(2):
        copy = halo(start.at[:, FACES[face]], halo_start.at[:, landing[face]], len(halos), face)
        copy.start()
        halos.append(copy)
    loads[5].wait()

    def fill(c, _):
        for face in range(2):
            halo_out[face, c] = direction[c, FACES[face]].astype(BF16)
        return 0

    lax.fori_loop(0, COLS, fill, 0)
    for face in range(2):
        copy = halo(halo_out.at[face], halo_in.at[:, landing[face]], len(halos), face)
        copy.start()
        halos.append(copy)

    def correlate(slot, first, planes):
        def body(x, total):
            for h in range(2):
                total = total + dot(
                    left[x, h].reshape(256, NZ),
                    wave[slot, :, x, pl.ds(h * HALF, HALF), :].reshape(128, NZ),
                    ((1,), (1,)),
                )
            return total

        return lax.fori_loop(
            first, first + planes, body, jnp.zeros((256, 128), F32), unroll=planes <= HALO
        )

    loads[4].wait()
    acc[:, 0:128] = correlate(0, 0, XS)

    forwards = []
    low_up.wait_recv()
    for q, part in enumerate(PIECES):
        copy = ring(wave.at[1, low, part], wave.at[2, low, part], 4 + 2 * q, up)
        copy.start()
        forwards.append(copy)
    high_down.wait_recv()
    for q, part in enumerate(PIECES):
        copy = ring(wave.at[3, high, part], wave.at[2, high, part], 5 + 2 * q, down)
        copy.start()
        forwards.append(copy)
    send_faces(1, low)
    send_faces(3, high)
    high_up.wait_recv()
    send_faces(1, high)
    low_down.wait_recv()
    send_faces(3, low)
    acc[:, 128:256] = correlate(1, 0, XS)
    acc[:, 384:512] = correlate(3, 0, XS)
    for q, part in enumerate(PIECES):
        forwards[q].wait_recv()
        forwards[len(PIECES) + q].wait_recv()
        if q < 2:
            send_face(2, pl.ds(0, BANDS), q, wave.at[2])
        term = correlate(2, part.start, part.size)
        acc[:, 256:384] = term if q == 0 else acc[:, 256:384] + term

    same = iota((256, 512), 0) % HALF == iota((256, 512), 1) % HALF
    folded = jnp.sum(jnp.where(same, acc[...], 0.0).reshape(16, HALF, 512), axis=1)
    pick = iota((512, 128), 0) // HALF
    lane = iota((512, 128), 1)
    mine = dot(
        folded[:8], jnp.where(pick == lane, 1.0, 0.0), precision=lax.Precision.HIGHEST
    ) + dot(
        folded[8:], jnp.where(pick + 32 == lane, 1.0, 0.0), precision=lax.Precision.HIGHEST
    )
    lane = iota((8, 128), 1)
    own = jnp.sum(jnp.sum(partial[...], axis=1), axis=1, keepdims=True)
    mine = mine + jnp.where(lane == 64, own, 0.0)

    def add_over_grid(table, value, k):
        table[g] = value

        for i in range(1, groups):
            pltpu.make_async_remote_copy(
                src_ref=table.at[g],
                dst_ref=table.at[g],
                send_sem=sum_send.at[k],
                recv_sem=sum_recv.at[k],
                device_id=(lax.rem(g + i, groups), z),
                device_id_type=MESH,
            ).start()
        others = table.at[pl.ds(0, groups - 1)]
        pltpu.make_async_copy(others, others, sum_recv.at[k]).wait()
        total = jnp.sum(table[...], axis=0)
        pltpu.make_async_copy(others, others, sum_send.at[k]).wait()
        return total

    total = add_over_grid(sums, mine, 0)

    for load in loads[6:]:
        load.wait()
    owner = lax.rem(z + jnp.where(lane < 8, 0, jnp.where(lane < 16, 3, jnp.where(lane < 24, 2, 1))), 4)
    column = iota((8, 128), 0)
    panel = jnp.zeros((8, 128), jnp.int32)
    old = jnp.zeros((8, 128), F32)
    for c in range(COLS):
        panel = jnp.where(column == c, panel_ref[c], panel)
        old = jnp.where(column == c, old_ref[c], old)
    cells = float(groups * XS * NY * NZ)
    chosen = jnp.where(
        jnp.logical_and(lane < 32, owner * BANDS // PB == panel), total, 0.0
    ) / cells
    overlap = pltpu.roll(total, 96, 1)
    rr = jnp.sum(
        jnp.where(lane == 64, total, 0.0) - chosen * overlap, axis=1, keepdims=True
    )
    rr = jnp.broadcast_to(rr, (8, 128))
    rr_out[...] = rr
    beta = rr / old

    top = chosen.astype(BF16)
    rest = (chosen - top.astype(F32)).astype(BF16)
    pair = jnp.concatenate([top.astype(F32), rest.astype(F32)], axis=0).astype(BF16)
    spread = dot(
        jnp.where(iota((256, 16), 0) // HALF == iota((256, 16), 1), 1.0, 0.0).astype(BF16), pair
    ).astype(BF16)
    spread = dot(
        spread,
        jnp.where(iota((128, 512), 1) // HALF == iota((128, 512), 0), 1.0, 0.0).astype(BF16),
    )
    kron[...] = jnp.where(same, spread, 0.0).astype(BF16)

    def removed(source, x):
        plane = [
            source[:, :, x, h * HALF : (h + 1) * HALF, :].reshape(512, NZ) for h in range(2)
        ]
        both = dot(kron[...], jnp.concatenate(plane, axis=1))
        both = both[:128] + both[128:]
        return lambda c, h: both[c * HALF : (c + 1) * HALF, h * NZ : (h + 1) * NZ]

    for x in range(XS):
        gone = removed(wave, x)
        for c in range(COLS):
            for h in range(2):
                part = slice(h * HALF, (h + 1) * HALF)
                new_dir[c, x, part] = (
                    start[c, x, part] - gone(c, h) + beta[c : c + 1, :1] * direction[c, x, part]
                )
    for copy in halos:
        copy.wait_recv()
    for x in range(2 * HALO):
        gone = removed(halo_wave, x)
        for c in range(COLS):
            for h in range(2):
                part = slice(h * HALF, (h + 1) * HALF)
                halo_dir[c, x, part] = (
                    halo_start[c, x, part]
                    - gone(c, h)
                    + beta[c : c + 1, :1] * halo_in[c, x, part].astype(F32)
                ).astype(BF16)

    for c in range(COLS):
        value = new_dir[c].reshape(256, NZ)
        top = value.astype(BF16)
        beside = dot(
            sten[...], jnp.concatenate([top, halo_dir[c].reshape(192, NZ)], axis=0)
        ) + dot(top, sten_z[...])
        local = pot[...].reshape(256, NZ) - shift_of(c) - 1.5 * K0
        full = UNSCALE * beside + local * value
        image[c] = full.reshape(XS, NY, NZ)
        total = jnp.sum((full * value).reshape(32, 8, NZ), axis=0)
        partial[c] = total[:, :128] + total[:, 128:256] + total[:, 256:]
    curvature = jnp.sum(add_over_grid(curves, jnp.sum(partial[...], axis=1), 1), axis=1, keepdims=True)
    step_out[...] = rr / curvature

    for copy in (low_up, high_down, high_up, low_down, *forwards, *halos):
        copy.wait_send()


def last_kernel(
    step, rr, solution_in, residual_in, new_dir, image, solution_hbm, residual_hbm, dir_hbm, rr_out, solution_new, residual_new, sems
):
    copies = [pltpu.make_async_copy(new_dir, dir_hbm, sems.at[2 * COLS])]
    copies[0].start()
    lane, row = iota((8, 128), 1), iota((8, 128), 0)
    rr_out[...] = jnp.sum(jnp.where(lane == row, rr[...], 0.0), axis=0)[:COLS]
    for c in range(COLS):
        alpha = step[c : c + 1, :1]
        solution_new[c] = solution_in[c] + alpha * new_dir[c]
        residual_new[c] = residual_in[c] - alpha * image[c]
        for i, (src, dst) in enumerate(((solution_new, solution_hbm), (residual_new, residual_hbm))):
            copy = pltpu.make_async_copy(src.at[c], dst.at[c], sems.at[2 * c + i])
            copy.start()
            copies.append(copy)
    for copy in copies:
        copy.wait()


def on_device(groups, residual, direction, solution, old_product, orbitals, energies, potential, column_index, panel_index):
    field = (COLS, XS, NY, NZ)
    hbm = pl.BlockSpec(memory_space=pltpu.HBM)
    vmem = pl.BlockSpec(memory_space=pltpu.VMEM)
    dma = pltpu.SemaphoreType.DMA
    new_dir, image, rr, step = pl.pallas_call(
        functools.partial(first_kernel, groups),
        out_shape=(
            jax.ShapeDtypeStruct(field, F32),
            jax.ShapeDtypeStruct(field, F32),
            jax.ShapeDtypeStruct((8, 128), F32),
            jax.ShapeDtypeStruct((8, 128), F32),
        ),
        in_specs=[hbm] * 8,
        out_specs=(vmem, vmem, vmem, vmem),
        scratch_shapes=[
            pltpu.VMEM(field, F32),
            pltpu.VMEM(field, F32),
            pltpu.VMEM((XS, NY, NZ), F32),
            pltpu.VMEM((4, BANDS, XS, NY, NZ), BF16),
            pltpu.VMEM((XS, 2, 2, COLS, HALF, NZ), BF16),
            pltpu.VMEM((256, 512), F32),
            pltpu.VMEM((256, 512), BF16),
            pltpu.VMEM((256, 448), BF16),
            pltpu.VMEM((NZ, NZ), BF16),
            pltpu.VMEM((4, BANDS, 2 * HALO, NY, NZ), BF16),
            pltpu.VMEM((2, COLS, HALO, NY, NZ), BF16),
            pltpu.VMEM((COLS, 2 * HALO, NY, NZ), F32),
            pltpu.VMEM((COLS, 2 * HALO, NY, NZ), BF16),
            pltpu.VMEM((COLS, 2 * HALO, NY, NZ), BF16),
            pltpu.VMEM((groups, 8, 128), F32),
            pltpu.VMEM((groups, 8, 128), F32),
            pltpu.VMEM((COLS, 8, 128), F32),
            pltpu.SMEM((COLS,), F32),
            pltpu.SMEM((32,), F32),
            pltpu.SMEM((COLS,), jnp.int32),
            pltpu.SMEM((COLS,), jnp.int32),
            dma((8,)),
            dma((4 + 2 * len(PIECES),)),
            dma((4 + 2 * len(PIECES),)),
            dma((2,)),
            dma((2,)),
            dma((16,)),
            dma((16,)),
        ],
        compiler_params=pltpu.CompilerParams(
            collective_id=0, has_side_effects=True, vmem_limit_bytes=38 << 20
        ),
        name="project_and_apply",
    )(
        *(
            pltpu.with_memory_space_constraint(operand, pltpu.HBM)
            for operand in (
                residual,
                direction,
                orbitals,
                potential,
                old_product,
                energies,
                column_index,
                panel_index,
            )
        )
    )

    new_solution, new_residual, out_dir, new_product = pl.pallas_call(
        last_kernel,
        out_shape=(*(jax.ShapeDtypeStruct(field, F32) for _ in range(3)), jax.ShapeDtypeStruct((COLS,), F32)),
        in_specs=[vmem] * 6,
        out_specs=(hbm, hbm, hbm, vmem),
        scratch_shapes=[pltpu.VMEM(field, F32), pltpu.VMEM(field, F32), dma((2 * COLS + 1,))],
        compiler_params=pltpu.CompilerParams(vmem_limit_bytes=8 << 20),
        name="take_step",
    )(step, rr, solution, residual, new_dir, image)
    return new_solution, new_residual, out_dir, new_product


def solution(mesh):
    field = P("band", "grid", None, None)
    return jax.shard_map(
        functools.partial(on_device, mesh.shape["grid"]),
        mesh=mesh,
        in_specs=(
            field,
            field,
            field,
            P("band"),
            field,
            P(),
            P("grid", None, None),
            P("band"),
            P("band"),
        ),
        out_specs=(field, field, field, P("band")),
        check_vma=False,
    )
```

```python
import functools

import jax
import jax.numpy as jnp
from jax import lax
from jax.experimental import pallas as pl
from jax.experimental.pallas import tpu as pltpu
from jax.sharding import PartitionSpec as P

MESH = pl.DeviceIdType.MESH
F32 = jnp.float32
BF16 = jnp.bfloat16

PB = 16
K0, K1, K2, K3 = (-49.0 / 18.0, 3.0 / 2.0, -3.0 / 20.0, 1.0 / 90.0)
SCALED = (135.0, -13.5, 1.0)
UNSCALE = -0.5 / 90.0

COLS = 8
BANDS = 8
XS = 8
NY = 32
NZ = 384
HALF = 16
HALO = 3
FACES = (pl.ds(0, HALO), pl.ds(XS - HALO, HALO))
PIECES = (pl.ds(0, 2), pl.ds(XS - 2, 2), pl.ds(2, 1), pl.ds(XS - 3, 1), pl.ds(HALO, XS - 2 * HALO))
TURNS = 4


def iota(shape, dim):
    return lax.broadcasted_iota(jnp.int32, shape, dim)


def coefficient(distance):
    gap = jnp.abs(distance)
    return jnp.where(
        gap == 1, SCALED[0], jnp.where(gap == 2, SCALED[1], jnp.where(gap == 3, SCALED[2], 0.0))
    )


def dot(left, right, dims=((1,), (0,)), precision=None):
    return lax.dot_general(
        left, right, (dims, ((), ())), precision=precision, preferred_element_type=F32
    )


def first_kernel(
    groups,
    res_hbm,
    dir_hbm,
    orb_hbm,
    pot_hbm,
    old_hbm,
    energy_hbm,
    column_hbm,
    panel_hbm,
    new_dir,
    image,
    rr_out,
    step_out,
    start,
    direction,
    pot,
    wave,
    left,
    kron,
    sten,
    sten_z,
    halo_wave,
    halo_out,
    halo_start,
    halo_in,
    halo_dir,
    sums,
    curves,
    partial,
    old_ref,
    energy_ref,
    column_ref,
    panel_ref,
    local_sem,
    ring_send,
    ring_recv,
    sum_send,
    sum_recv,
    halo_send,
    halo_recv,
):
    g = lax.axis_index("grid")
    z = lax.axis_index("band")
    up, down = lax.rem(z + 1, 4), lax.rem(z + 3, 4)

    loads = [
        pltpu.make_async_copy(src, dst, local_sem.at[i])
        for i, (src, dst) in enumerate(
            (
                (column_hbm, column_ref),
                (energy_hbm, energy_ref),
                (pot_hbm, pot),
                (res_hbm, start),
                (orb_hbm, wave.at[0]),
                (dir_hbm, direction),
                (old_hbm, old_ref),
                (panel_hbm, panel_ref),
            )
        )
    ]
    barrier = pltpu.get_barrier_semaphore()
    for to in (up, down):
        pl.semaphore_signal(barrier, inc=1, device_id=(g, to), device_id_type=MESH)

    for k in range(1, groups):
        pl.semaphore_signal(
            barrier, inc=1, device_id=(lax.rem(g + k, groups), z), device_id_type=MESH
        )
    for load in loads:
        load.start()
    pl.semaphore_wait(barrier, groups + 1)

    def ring(src, dst, i, to):
        return pltpu.make_async_remote_copy(
            src_ref=src,
            dst_ref=dst,
            send_sem=ring_send.at[i],
            recv_sem=ring_recv.at[i],
            device_id=(g, to),
            device_id_type=MESH,
        )

    sides = (lax.rem(g + groups - 1, groups), lax.rem(g + 1, groups))

    def halo(src, dst, i, face):
        return pltpu.make_async_remote_copy(
            src_ref=src,
            dst_ref=dst,
            send_sem=halo_send.at[i],
            recv_sem=halo_recv.at[i],
            device_id=(sides[face], z),
            device_id_type=MESH,
        )

    landing = (pl.ds(HALO, HALO), pl.ds(0, HALO))
    halos = []

    def send_faces(slot, bands, src=None):
        src = wave.at[slot] if src is None else src
        for face in range(2):
            send_face(slot, bands, face, src, FACES[face], landing[face])

    def send_face(slot, bands, face, src, planes, place):
        copy = halo(src.at[bands, planes], halo_wave.at[slot, bands, place], len(halos), face)
        copy.start()
        halos.append(copy)

    low, high = pl.ds(0, BANDS // 2), pl.ds(BANDS // 2, BANDS // 2)
    low_up = ring(orb_hbm.at[low], wave.at[1, low], 0, up)
    high_down = ring(orb_hbm.at[high], wave.at[3, high], 1, down)
    high_up = ring(orb_hbm.at[high], wave.at[1, high], 2, up)
    low_down = ring(orb_hbm.at[low], wave.at[3, low], 3, down)
    low_up.start()
    high_down.start()
    high_up.start()
    low_down.start()
    send_faces(0, pl.ds(0, BANDS), orb_hbm)

    rows, cols = iota((256, 448), 0), iota((256, 448), 1)
    plane = cols // NY
    there = jnp.where(plane < XS, plane, jnp.where(plane < XS + HALO, plane - XS - HALO, plane - HALO))
    inside = jnp.where(plane < XS, 1, jnp.where(plane < XS + HALO, g, groups - 1 - g)) > 0
    dx, dy = rows // NY - there, rows % NY - cols % NY
    weight = jnp.where(dy == 0, coefficient(dx), jnp.where(dx == 0, coefficient(dy), 0.0))
    sten[...] = jnp.where(inside, weight, 0.0).astype(BF16)
    sten_z[...] = coefficient(iota((NZ, NZ), 0) - iota((NZ, NZ), 1)).astype(BF16)

    def shift_of(c):
        return energy_ref[column_ref[c] // 3]

    for load in loads[:4]:
        load.wait()

    def start_column(c, _):
        e = shift_of(c)

        def start_plane(x, total):
            r = start[c, x]
            s = r / (pot[x] - e - 1.5 * K0)
            start[c, x] = s
            for h in range(2):
                part = slice(h * HALF, (h + 1) * HALF)
                left[x, h, 0, c] = s[part].astype(BF16)
                left[x, h, 1, c] = r[part].astype(BF16)
            return total + jnp.sum((r * s).reshape(4, 8, NZ), axis=0)

        total = lax.fori_loop(0, XS, start_plane, jnp.zeros((8, NZ), F32))
        partial[c] = total[:, :128] + total[:, 128:256] + total[:, 256:]
        return 0

    lax.fori_loop(0, COLS, start_column, 0)
    for face in range(2):
        copy = halo(start.at[:, FACES[face]], halo_start.at[:, landing[face]], len(halos), face)
        copy.start()
        halos.append(copy)
    loads[5].wait()

    def fill(c, _):
        for face in range(2):
            halo_out[face, c] = direction[c, FACES[face]].astype(BF16)
        return 0

    lax.fori_loop(0, COLS, fill, 0)
    for face in range(2):
        copy = halo(halo_out.at[face], halo_in.at[:, landing[face]], len(halos), face)
        copy.start()
        halos.append(copy)

    def correlate(slot, first, planes):
        def body(x, total):
            for h in range(2):
                total = total + dot(
                    left[x, h].reshape(256, NZ),
                    wave[slot, :, x, pl.ds(h * HALF, HALF), :].reshape(128, NZ),
                    ((1,), (1,)),
                )
            return total

        return lax.fori_loop(
            first, first + planes, body, jnp.zeros((256, 128), F32), unroll=planes <= HALO
        )

    lane = iota((8, 128), 1)
    own = jnp.sum(jnp.sum(partial[...], axis=1), axis=1, keepdims=True)
    same = iota((256, 128), 0) % HALF == iota((256, 128), 1) % HALF

    def fold(block, slot):
        rows = jnp.sum(jnp.where(same, block, 0.0).reshape(16, HALF, 128), axis=1)
        high = rows.astype(BF16).astype(F32)
        middle = (rows - high).astype(BF16).astype(F32)
        terms = jnp.concatenate([high, middle, rows - high - middle], axis=0).astype(BF16)
        pick = iota((128, 128), 0) // HALF + slot * BANDS
        ones = jnp.where(pick == iota((128, 128), 1), 1.0, 0.0).astype(BF16)
        parts = dot(terms, ones)
        parts = parts[:16] + parts[16:32] + parts[32:]
        return parts[:8] + pltpu.roll(parts[8:], 32, 1)

    loads[4].wait()
    mine = fold(correlate(0, 0, XS), 0)

    forwards = []
    low_up.wait_recv()
    for q, part in enumerate(PIECES):
        copy = ring(wave.at[1, low, part], wave.at[2, low, part], 4 + 2 * q, up)
        copy.start()
        forwards.append(copy)
    high_down.wait_recv()
    for q, part in enumerate(PIECES):
        copy = ring(wave.at[3, high, part], wave.at[2, high, part], 5 + 2 * q, down)
        copy.start()
        forwards.append(copy)
    send_faces(1, low)
    send_faces(3, high)
    high_up.wait_recv()
    send_faces(1, high)
    low_down.wait_recv()
    send_faces(3, low)
    mine = mine + fold(correlate(1, 0, XS), 1)
    mine = mine + fold(correlate(3, 0, XS), 3)
    mine = mine + jnp.where(lane == 64, own, 0.0)
    for q, part in enumerate(PIECES):
        forwards[q].wait_recv()
        forwards[len(PIECES) + q].wait_recv()
        if q < TURNS:
            place = pl.ds(part.start + (HALO if q % 2 == 0 else HALO - XS), part.size)
            send_face(2, pl.ds(0, BANDS), q % 2, wave.at[2], part, place)
        term = correlate(2, part.start, part.size)
        last = term if q == 0 else last + term
    mine = mine + fold(last, 2)

    def far(i):
        steps = (i // 8, i // 2 % 4)
        return -sum(min(n, 4 - n) for n in steps)

    order = sorted(range(1, groups), key=far)

    def add_over_grid(table, value, k):
        table[g] = value

        for i in order:
            pltpu.make_async_remote_copy(
                src_ref=table.at[g],
                dst_ref=table.at[g],
                send_sem=sum_send.at[k],
                recv_sem=sum_recv.at[k],
                device_id=(lax.rem(g + i, groups), z),
                device_id_type=MESH,
            ).start()
        others = table.at[pl.ds(0, groups - 1)]
        pltpu.make_async_copy(others, others, sum_recv.at[k]).wait()
        return jnp.sum(table[...], axis=0)

    total = add_over_grid(sums, mine, 0)

    for load in loads[6:]:
        load.wait()
    owner = lax.rem(z + jnp.where(lane < 8, 0, jnp.where(lane < 16, 3, jnp.where(lane < 24, 2, 1))), 4)
    column = iota((8, 128), 0)
    panel = jnp.zeros((8, 128), jnp.int32)
    old = jnp.zeros((8, 128), F32)
    for c in range(COLS):
        panel = jnp.where(column == c, panel_ref[c], panel)
        old = jnp.where(column == c, old_ref[c], old)
    cells = float(groups * XS * NY * NZ)
    chosen = jnp.where(
        jnp.logical_and(lane < 32, owner * BANDS // PB == panel), total, 0.0
    ) / cells
    overlap = pltpu.roll(total, 96, 1)
    rr = jnp.sum(
        jnp.where(lane == 64, total, 0.0) - chosen * overlap, axis=1, keepdims=True
    )
    rr = jnp.broadcast_to(rr, (8, 128))
    rr_out[...] = rr
    beta = rr / old

    top = chosen.astype(BF16)
    rest = (chosen - top.astype(F32)).astype(BF16)
    pair = jnp.concatenate([top.astype(F32), rest.astype(F32)], axis=0).astype(BF16)
    spread = dot(
        pair,
        jnp.where(iota((128, 512), 1) // HALF == iota((128, 512), 0), 1.0, 0.0).astype(BF16),
    )
    spread = jnp.broadcast_to(spread[:, None, :], (16, HALF, 512)).reshape(256, 512)
    same = iota((256, 512), 0) % HALF == iota((256, 512), 1) % HALF
    kron[...] = jnp.where(same, spread, 0.0).astype(BF16)

    def removed(source, x):
        plane = [
            source[:, :, x, h * HALF : (h + 1) * HALF, :].reshape(512, NZ) for h in range(2)
        ]
        both = dot(kron[...], jnp.concatenate(plane, axis=1))
        both = both[:128] + both[128:]
        return lambda c, h: both[c * HALF : (c + 1) * HALF, h * NZ : (h + 1) * NZ]

    for x in range(XS):
        gone = removed(wave, x)
        for c in range(COLS):
            for h in range(2):
                part = slice(h * HALF, (h + 1) * HALF)
                new_dir[c, x, part] = (
                    start[c, x, part] - gone(c, h) + beta[c : c + 1, :1] * direction[c, x, part]
                )
    for copy in halos:
        copy.wait_recv()
    for x in range(2 * HALO):
        gone = removed(halo_wave, x)
        for c in range(COLS):
            for h in range(2):
                part = slice(h * HALF, (h + 1) * HALF)
                halo_dir[c, x, part] = (
                    halo_start[c, x, part]
                    - gone(c, h)
                    + beta[c : c + 1, :1] * halo_in[c, x, part].astype(F32)
                ).astype(BF16)

    for c in range(COLS):
        value = new_dir[c].reshape(256, NZ)
        top = value.astype(BF16)
        beside = dot(
            sten[...], jnp.concatenate([top, halo_dir[c].reshape(192, NZ)], axis=0)
        ) + dot(top, sten_z[...])
        local = pot[...].reshape(256, NZ) - shift_of(c) - 1.5 * K0
        full = UNSCALE * beside + local * value
        image[c] = full.reshape(XS, NY, NZ)
        total = jnp.sum((full * value).reshape(32, 8, NZ), axis=0)
        partial[c] = total[:, :128] + total[:, 128:256] + total[:, 256:]
    curvature = jnp.sum(add_over_grid(curves, jnp.sum(partial[...], axis=1), 1), axis=1, keepdims=True)
    step_out[...] = rr / curvature

    for k, table in enumerate((sums, curves)):
        others = table.at[pl.ds(0, groups - 1)]
        pltpu.make_async_copy(others, others, sum_send.at[k]).wait()
    for copy in (low_up, high_down, high_up, low_down, *forwards, *halos):
        copy.wait_send()


def last_kernel(
    step, rr, solution_in, residual_in, new_dir, image, solution_hbm, residual_hbm, dir_hbm, rr_out, solution_new, residual_new, sems
):
    copies = [pltpu.make_async_copy(new_dir, dir_hbm, sems.at[2 * COLS])]
    copies[0].start()
    lane, row = iota((8, 128), 1), iota((8, 128), 0)
    rr_out[...] = jnp.sum(jnp.where(lane == row, rr[...], 0.0), axis=0)[:COLS]
    for c in range(COLS):
        alpha = step[c : c + 1, :1]
        solution_new[c] = solution_in[c] + alpha * new_dir[c]
        residual_new[c] = residual_in[c] - alpha * image[c]
        for i, (src, dst) in enumerate(((solution_new, solution_hbm), (residual_new, residual_hbm))):
            copy = pltpu.make_async_copy(src.at[c], dst.at[c], sems.at[2 * c + i])
            copy.start()
            copies.append(copy)
    for copy in copies:
        copy.wait()


def on_device(groups, residual, direction, solution, old_product, orbitals, energies, potential, column_index, panel_index):
    field = (COLS, XS, NY, NZ)
    hbm = pl.BlockSpec(memory_space=pltpu.HBM)
    vmem = pl.BlockSpec(memory_space=pltpu.VMEM)
    dma = pltpu.SemaphoreType.DMA
    new_dir, image, rr, step = pl.pallas_call(
        functools.partial(first_kernel, groups),
        out_shape=(
            jax.ShapeDtypeStruct(field, F32),
            jax.ShapeDtypeStruct(field, F32),
            jax.ShapeDtypeStruct((8, 128), F32),
            jax.ShapeDtypeStruct((8, 128), F32),
        ),
        in_specs=[hbm] * 8,
        out_specs=(vmem, vmem, vmem, vmem),
        scratch_shapes=[
            pltpu.VMEM(field, F32),
            pltpu.VMEM(field, F32),
            pltpu.VMEM((XS, NY, NZ), F32),
            pltpu.VMEM((4, BANDS, XS, NY, NZ), BF16),
            pltpu.VMEM((XS, 2, 2, COLS, HALF, NZ), BF16),
            pltpu.VMEM((256, 512), BF16),
            pltpu.VMEM((256, 448), BF16),
            pltpu.VMEM((NZ, NZ), BF16),
            pltpu.VMEM((4, BANDS, 2 * HALO, NY, NZ), BF16),
            pltpu.VMEM((2, COLS, HALO, NY, NZ), BF16),
            pltpu.VMEM((COLS, 2 * HALO, NY, NZ), F32),
            pltpu.VMEM((COLS, 2 * HALO, NY, NZ), BF16),
            pltpu.VMEM((COLS, 2 * HALO, NY, NZ), BF16),
            pltpu.VMEM((groups, 8, 128), F32),
            pltpu.VMEM((groups, 8, 128), F32),
            pltpu.VMEM((COLS, 8, 128), F32),
            pltpu.SMEM((COLS,), F32),
            pltpu.SMEM((32,), F32),
            pltpu.SMEM((COLS,), jnp.int32),
            pltpu.SMEM((COLS,), jnp.int32),
            dma((8,)),
            dma((4 + 2 * len(PIECES),)),
            dma((4 + 2 * len(PIECES),)),
            dma((2,)),
            dma((2,)),
            dma((14 + TURNS,)),
            dma((14 + TURNS,)),
        ],
        compiler_params=pltpu.CompilerParams(
            collective_id=0, has_side_effects=True, vmem_limit_bytes=38 << 20
        ),
        name="project_and_apply",
    )(
        *(
            pltpu.with_memory_space_constraint(operand, pltpu.HBM)
            for operand in (
                residual,
                direction,
                orbitals,
                potential,
                old_product,
                energies,
                column_index,
                panel_index,
            )
        )
    )

    new_solution, new_residual, out_dir, new_product = pl.pallas_call(
        last_kernel,
        out_shape=(*(jax.ShapeDtypeStruct(field, F32) for _ in range(3)), jax.ShapeDtypeStruct((COLS,), F32)),
        in_specs=[vmem] * 6,
        out_specs=(hbm, hbm, hbm, vmem),
        scratch_shapes=[pltpu.VMEM(field, F32), pltpu.VMEM(field, F32), dma((2 * COLS + 1,))],
        compiler_params=pltpu.CompilerParams(vmem_limit_bytes=8 << 20),
        name="take_step",
    )(step, rr, solution, residual, new_dir, image)
    return new_solution, new_residual, out_dir, new_product


def solution(mesh):
    field = P("band", "grid", None, None)
    return jax.shard_map(
        functools.partial(on_device, mesh.shape["grid"]),
        mesh=mesh,
        in_specs=(
            field,
            field,
            field,
            P("band"),
            field,
            P(),
            P("grid", None, None),
            P("band"),
            P("band"),
        ),
        out_specs=(field, field, field, P("band")),
        check_vma=False,
    )
```

```python
import functools

import jax
import jax.numpy as jnp
from jax import lax
from jax.experimental import pallas as pl
from jax.experimental.pallas import tpu as pltpu
from jax.sharding import PartitionSpec as P

MESH = pl.DeviceIdType.MESH
F32 = jnp.float32
BF16 = jnp.bfloat16

PB = 16
K0, K1, K2, K3 = (-49.0 / 18.0, 3.0 / 2.0, -3.0 / 20.0, 1.0 / 90.0)
SCALED = (135.0, -13.5, 1.0)
UNSCALE = -0.5 / 90.0

COLS = 8
BANDS = 8
XS = 8
NY = 32
NZ = 384
HALF = 16
HALO = 3
FACES = (pl.ds(0, HALO), pl.ds(XS - HALO, HALO))
PIECES = (pl.ds(0, 2), pl.ds(XS - 2, 2), pl.ds(2, 1), pl.ds(XS - 3, 1), pl.ds(HALO, XS - 2 * HALO))
TURNS = 4


def iota(shape, dim):
    return lax.broadcasted_iota(jnp.int32, shape, dim)


def coefficient(distance):
    gap = jnp.abs(distance)
    return jnp.where(
        gap == 1, SCALED[0], jnp.where(gap == 2, SCALED[1], jnp.where(gap == 3, SCALED[2], 0.0))
    )


def dot(left, right, dims=((1,), (0,)), precision=None):
    return lax.dot_general(
        left, right, (dims, ((), ())), precision=precision, preferred_element_type=F32
    )


def first_kernel(
    groups,
    res_hbm,
    dir_hbm,
    orb_hbm,
    pot_hbm,
    old_hbm,
    energy_hbm,
    column_hbm,
    panel_hbm,
    solution_hbm,
    new_dir,
    image,
    rr_out,
    step_out,
    residual_near,
    solution_near,
    start,
    direction,
    pot,
    wave,
    left,
    kron,
    kron_mask,
    kron_ones,
    sten,
    sten_z,
    halo_wave,
    halo_out,
    halo_start,
    halo_in,
    halo_dir,
    sums,
    curves,
    partial,
    old_ref,
    energy_ref,
    column_ref,
    panel_ref,
    local_sem,
    ring_send,
    ring_recv,
    sum_send,
    sum_recv,
    halo_send,
    halo_recv,
):
    g = lax.axis_index("grid")
    z = lax.axis_index("band")
    up, down = lax.rem(z + 1, 4), lax.rem(z + 3, 4)

    loads = [
        pltpu.make_async_copy(src, dst, local_sem.at[i])
        for i, (src, dst) in enumerate(
            (
                (column_hbm, column_ref),
                (energy_hbm, energy_ref),
                (pot_hbm, pot),
                (res_hbm, start),
                (orb_hbm, wave.at[0]),
                (dir_hbm, direction),
                (old_hbm, old_ref),
                (panel_hbm, panel_ref),
                (res_hbm, residual_near),
                (solution_hbm, solution_near),
            )
        )
    ]
    barrier = pltpu.get_barrier_semaphore()
    for to in (up, down):
        pl.semaphore_signal(barrier, inc=1, device_id=(g, to), device_id_type=MESH)

    for k in range(1, groups):
        pl.semaphore_signal(
            barrier, inc=1, device_id=(lax.rem(g + k, groups), z), device_id_type=MESH
        )
    pl.semaphore_wait(barrier, groups + 1)

    def ring(src, dst, i, to):
        return pltpu.make_async_remote_copy(
            src_ref=src,
            dst_ref=dst,
            send_sem=ring_send.at[i],
            recv_sem=ring_recv.at[i],
            device_id=(g, to),
            device_id_type=MESH,
        )

    sides = (lax.rem(g + groups - 1, groups), lax.rem(g + 1, groups))

    def halo(src, dst, i, face):
        return pltpu.make_async_remote_copy(
            src_ref=src,
            dst_ref=dst,
            send_sem=halo_send.at[i],
            recv_sem=halo_recv.at[i],
            device_id=(sides[face], z),
            device_id_type=MESH,
        )

    landing = (pl.ds(HALO, HALO), pl.ds(0, HALO))
    halos = []

    def send_faces(slot, bands, src=None):
        src = wave.at[slot] if src is None else src
        for face in range(2):
            send_face(slot, bands, face, src, FACES[face], landing[face])

    def send_face(slot, bands, face, src, planes, place):
        copy = halo(src.at[bands, planes], halo_wave.at[slot, bands, place], len(halos), face)
        copy.start()
        halos.append(copy)

    low, high = pl.ds(0, BANDS // 2), pl.ds(BANDS // 2, BANDS // 2)
    low_up = ring(orb_hbm.at[low], wave.at[1, low], 0, up)
    high_down = ring(orb_hbm.at[high], wave.at[3, high], 1, down)
    high_up = ring(orb_hbm.at[high], wave.at[1, high], 2, up)
    low_down = ring(orb_hbm.at[low], wave.at[3, low], 3, down)
    low_up.start()
    high_down.start()
    high_up.start()
    low_down.start()
    for load in loads[:5]:
        load.start()
    rows, cols = iota((256, 448), 0), iota((256, 448), 1)
    plane = cols // NY
    there = jnp.where(plane < XS, plane, jnp.where(plane < XS + HALO, plane - XS - HALO, plane - HALO))
    inside = jnp.where(plane < XS, 1, jnp.where(plane < XS + HALO, g, groups - 1 - g)) > 0
    dx, dy = rows // NY - there, rows % NY - cols % NY
    weight = jnp.where(dy == 0, coefficient(dx), jnp.where(dx == 0, coefficient(dy), 0.0))
    sten[...] = jnp.where(inside, weight, 0.0).astype(BF16)
    sten_z[...] = coefficient(iota((NZ, NZ), 0) - iota((NZ, NZ), 1)).astype(BF16)

    def shift_of(c):
        return energy_ref[column_ref[c] // 3]

    for load in loads[:4]:
        load.wait()

    def start_column(c, _):
        e = shift_of(c)

        def start_plane(x, total):
            r = start[c, x]
            s = r / (pot[x] - e - 1.5 * K0)
            start[c, x] = s
            for h in range(2):
                part = slice(h * HALF, (h + 1) * HALF)
                left[x, h, 0, c] = s[part].astype(BF16)
                left[x, h, 1, c] = r[part].astype(BF16)
            return total + jnp.sum((r * s).reshape(4, 8, NZ), axis=0)

        total = lax.fori_loop(0, XS, start_plane, jnp.zeros((8, NZ), F32))
        partial[c] = total[:, :128] + total[:, 128:256] + total[:, 256:]
        return 0

    for load in loads[5:]:
        load.start()
    lax.fori_loop(0, COLS, start_column, 0)
    send_faces(0, pl.ds(0, BANDS), orb_hbm)
    for face in range(2):
        copy = halo(start.at[:, FACES[face]], halo_start.at[:, landing[face]], len(halos), face)
        copy.start()
        halos.append(copy)
    loads[5].wait()

    def fill(c, _):
        for face in range(2):
            halo_out[face, c] = direction[c, FACES[face]].astype(BF16)
        return 0

    lax.fori_loop(0, COLS, fill, 0)
    for face in range(2):
        copy = halo(halo_out.at[face], halo_in.at[:, landing[face]], len(halos), face)
        copy.start()
        halos.append(copy)

    def correlate(slot, first, planes):
        def body(x, total):
            for h in range(2):
                total = total + dot(
                    left[x, h].reshape(256, NZ),
                    wave[slot, :, x, pl.ds(h * HALF, HALF), :].reshape(128, NZ),
                    ((1,), (1,)),
                )
            return total

        return lax.fori_loop(
            first, first + planes, body, jnp.zeros((256, 128), F32), unroll=planes <= HALO
        )

    lane = iota((8, 128), 1)
    own = jnp.sum(jnp.sum(partial[...], axis=1), axis=1, keepdims=True)
    same = iota((256, 128), 0) % HALF == iota((256, 128), 1) % HALF

    def fold(block, slot):
        rows = jnp.sum(jnp.where(same, block, 0.0).reshape(16, HALF, 128), axis=1)
        high = rows.astype(BF16).astype(F32)
        middle = (rows - high).astype(BF16).astype(F32)
        terms = jnp.concatenate([high, middle, rows - high - middle], axis=0).astype(BF16)
        pick = iota((128, 128), 0) // HALF + slot * BANDS
        ones = jnp.where(pick == iota((128, 128), 1), 1.0, 0.0).astype(BF16)
        parts = dot(terms, ones)
        parts = parts[:16] + parts[16:32] + parts[32:]
        return parts[:8] + pltpu.roll(parts[8:], 32, 1)

    loads[4].wait()
    mine = fold(correlate(0, 0, XS), 0)

    forwards = []
    low_up.wait_recv()
    for q, part in enumerate(PIECES):
        copy = ring(wave.at[1, low, part], wave.at[2, low, part], 4 + 2 * q, up)
        copy.start()
        forwards.append(copy)
    high_down.wait_recv()
    for q, part in enumerate(PIECES):
        copy = ring(wave.at[3, high, part], wave.at[2, high, part], 5 + 2 * q, down)
        copy.start()
        forwards.append(copy)
    send_faces(1, low)
    send_faces(3, high)
    high_up.wait_recv()
    send_faces(1, high)
    low_down.wait_recv()
    send_faces(3, low)
    mine = mine + fold(correlate(1, 0, XS), 1)
    mine = mine + fold(correlate(3, 0, XS), 3)
    mine = mine + jnp.where(lane == 64, own, 0.0)
    for q, part in enumerate(PIECES):
        forwards[q].wait_recv()
        forwards[len(PIECES) + q].wait_recv()
        if q < TURNS:
            place = pl.ds(part.start + (HALO if q % 2 == 0 else HALO - XS), part.size)
            send_face(2, pl.ds(0, BANDS), q % 2, wave.at[2], part, place)
        term = correlate(2, part.start, part.size)
        last = term if q == 0 else last + term
    mine = mine + fold(last, 2)

    def far(i):
        steps = (i // 8, i // 2 % 4)
        return -sum(min(n, 4 - n) for n in steps)

    order = sorted(range(1, groups), key=far)

    def send_over_grid(table, value, k):
        table[g] = value

        for i in order:
            pltpu.make_async_remote_copy(
                src_ref=table.at[g],
                dst_ref=table.at[g],
                send_sem=sum_send.at[k],
                recv_sem=sum_recv.at[k],
                device_id=(lax.rem(g + i, groups), z),
                device_id_type=MESH,
            ).start()
    def sum_over_grid(table, k):
        others = table.at[pl.ds(0, groups - 1)]
        pltpu.make_async_copy(others, others, sum_recv.at[k]).wait()
        return jnp.sum(table[...], axis=0)

    send_over_grid(sums, mine, 0)

    for load in loads[6:]:
        load.wait()
    owner = lax.rem(z + jnp.where(lane < 8, 0, jnp.where(lane < 16, 3, jnp.where(lane < 24, 2, 1))), 4)
    column = iota((8, 128), 0)
    panel = jnp.zeros((8, 128), jnp.int32)
    old = jnp.zeros((8, 128), F32)
    for c in range(COLS):
        panel = jnp.where(column == c, panel_ref[c], panel)
        old = jnp.where(column == c, old_ref[c], old)
    mask = jnp.where(iota((256, 512), 0) % HALF == iota((256, 512), 1) % HALF, 1.0, 0.0)
    kron_mask[...] = mask.astype(BF16)
    widen = jnp.where(iota((128, 512), 1) // HALF == iota((128, 512), 0), 1.0, 0.0)
    kron_ones[...] = widen.astype(BF16)
    member = jnp.logical_and(lane < 32, owner * BANDS // PB == panel)
    for copy in halos:
        copy.wait_recv()
    total = sum_over_grid(sums, 0)

    cells = float(groups * XS * NY * NZ)
    chosen = jnp.where(member, total, 0.0) / cells
    overlap = pltpu.roll(total, 96, 1)
    rr = jnp.sum(
        jnp.where(lane == 64, total, 0.0) - chosen * overlap, axis=1, keepdims=True
    )
    rr = jnp.broadcast_to(rr, (8, 128))
    rr_out[...] = rr
    beta = rr / old

    top = chosen.astype(BF16)
    rest = (chosen - top.astype(F32)).astype(BF16)
    pair = jnp.concatenate([top.astype(F32), rest.astype(F32)], axis=0).astype(BF16)
    spread = dot(pair, kron_ones[...])
    spread = jnp.broadcast_to(spread[:, None, :], (16, HALF, 512)).reshape(256, 512)
    kron[...] = spread.astype(BF16) * kron_mask[...]

    def removed(source, x):
        plane = [
            source[:, :, x, h * HALF : (h + 1) * HALF, :].reshape(512, NZ) for h in range(2)
        ]
        both = dot(kron[...], jnp.concatenate(plane, axis=1))
        both = both[:128] + both[128:]
        return lambda c, h: both[c * HALF : (c + 1) * HALF, h * NZ : (h + 1) * NZ]

    for x in range(XS):
        gone = removed(wave, x)
        for c in range(COLS):
            for h in range(2):
                part = slice(h * HALF, (h + 1) * HALF)
                new_dir[c, x, part] = (
                    start[c, x, part] - gone(c, h) + beta[c : c + 1, :1] * direction[c, x, part]
                )
    for x in range(2 * HALO):
        gone = removed(halo_wave, x)
        for c in range(COLS):
            for h in range(2):
                part = slice(h * HALF, (h + 1) * HALF)
                halo_dir[c, x, part] = (
                    halo_start[c, x, part]
                    - gone(c, h)
                    + beta[c : c + 1, :1] * halo_in[c, x, part].astype(F32)
                ).astype(BF16)

    for first in range(0, COLS, 2):
        pair = [new_dir[c].reshape(256, NZ) for c in (first, first + 1)]
        tops = [value.astype(BF16) for value in pair]
        around = [
            jnp.concatenate([top, halo_dir[first + i].reshape(192, NZ)], axis=0)
            for i, top in enumerate(tops)
        ]
        across = dot(sten[...], jnp.concatenate(around, axis=1))
        for i, (value, top) in enumerate(zip(pair, tops)):
            c = first + i
            along = [
                dot(top, sten_z[:, 0:256]),
                dot(top[:, 128:384], sten_z[128:384, 256:384]),
            ]
            beside = across[:, i * NZ : (i + 1) * NZ] + jnp.concatenate(along, axis=1)
            local = pot[...].reshape(256, NZ) - (shift_of(c) + 1.5 * K0)
            full = UNSCALE * beside + local * value
            image[c] = full.reshape(XS, NY, NZ)
            total = jnp.sum((full * value).reshape(32, 8, NZ), axis=0)
            partial[c] = total[:, :128] + total[:, 128:256] + total[:, 256:]
    send_over_grid(curves, jnp.sum(partial[...], axis=1), 1)

    def drain(table, k):
        others = table.at[pl.ds(0, groups - 1)]
        pltpu.make_async_copy(others, others, sum_send.at[k]).wait()

    drain(sums, 0)
    for copy in (low_up, high_down, high_up, low_down, *forwards, *halos):
        copy.wait_send()
    drain(curves, 1)
    curvature = jnp.sum(sum_over_grid(curves, 1), axis=1, keepdims=True)
    step_out[...] = rr / curvature


def last_kernel(
    step, rr, solution_in, residual_in, new_dir, image, solution_hbm, residual_hbm, dir_hbm, rr_out, solution_new, residual_new, sems
):
    copies = [pltpu.make_async_copy(new_dir, dir_hbm, sems.at[2 * COLS])]
    copies[0].start()
    lane, row = iota((8, 128), 1), iota((8, 128), 0)
    rr_out[...] = jnp.sum(jnp.where(lane == row, rr[...], 0.0), axis=0)[:COLS]
    for c in range(COLS):
        alpha = step[c : c + 1, :1]
        solution_new[c] = solution_in[c] + alpha * new_dir[c]
        residual_new[c] = residual_in[c] - alpha * image[c]
        for i, (src, dst) in enumerate(((solution_new, solution_hbm), (residual_new, residual_hbm))):
            copy = pltpu.make_async_copy(src.at[c], dst.at[c], sems.at[2 * c + i])
            copy.start()
            copies.append(copy)
    for copy in copies:
        copy.wait()


def on_device(groups, residual, direction, solution, old_product, orbitals, energies, potential, column_index, panel_index):
    field = (COLS, XS, NY, NZ)
    hbm = pl.BlockSpec(memory_space=pltpu.HBM)
    vmem = pl.BlockSpec(memory_space=pltpu.VMEM)
    dma = pltpu.SemaphoreType.DMA
    new_dir, image, rr, step, residual, solution = pl.pallas_call(
        functools.partial(first_kernel, groups),
        out_shape=(
            jax.ShapeDtypeStruct(field, F32),
            jax.ShapeDtypeStruct(field, F32),
            jax.ShapeDtypeStruct((8, 128), F32),
            jax.ShapeDtypeStruct((8, 128), F32),
            jax.ShapeDtypeStruct(field, F32),
            jax.ShapeDtypeStruct(field, F32),
        ),
        in_specs=[hbm] * 9,
        out_specs=(vmem,) * 6,
        scratch_shapes=[
            pltpu.VMEM(field, F32),
            pltpu.VMEM(field, F32),
            pltpu.VMEM((XS, NY, NZ), F32),
            pltpu.VMEM((4, BANDS, XS, NY, NZ), BF16),
            pltpu.VMEM((XS, 2, 2, COLS, HALF, NZ), BF16),
            pltpu.VMEM((256, 512), BF16),
            pltpu.VMEM((256, 512), BF16),
            pltpu.VMEM((128, 512), BF16),
            pltpu.VMEM((256, 448), BF16),
            pltpu.VMEM((NZ, NZ), BF16),
            pltpu.VMEM((4, BANDS, 2 * HALO, NY, NZ), BF16),
            pltpu.VMEM((2, COLS, HALO, NY, NZ), BF16),
            pltpu.VMEM((COLS, 2 * HALO, NY, NZ), F32),
            pltpu.VMEM((COLS, 2 * HALO, NY, NZ), BF16),
            pltpu.VMEM((COLS, 2 * HALO, NY, NZ), BF16),
            pltpu.VMEM((groups, 8, 128), F32),
            pltpu.VMEM((groups, 8, 128), F32),
            pltpu.VMEM((COLS, 8, 128), F32),
            pltpu.SMEM((COLS,), F32),
            pltpu.SMEM((32,), F32),
            pltpu.SMEM((COLS,), jnp.int32),
            pltpu.SMEM((COLS,), jnp.int32),
            dma((10,)),
            dma((4 + 2 * len(PIECES),)),
            dma((4 + 2 * len(PIECES),)),
            dma((2,)),
            dma((2,)),
            dma((14 + TURNS,)),
            dma((14 + TURNS,)),
        ],
        compiler_params=pltpu.CompilerParams(
            collective_id=0, has_side_effects=True, vmem_limit_bytes=38 << 20
        ),
        name="project_and_apply",
    )(
        *(
            pltpu.with_memory_space_constraint(operand, pltpu.HBM)
            for operand in (
                residual,
                direction,
                orbitals,
                potential,
                old_product,
                energies,
                column_index,
                panel_index,
                solution,
            )
        )
    )

    new_solution, new_residual, out_dir, new_product = pl.pallas_call(
        last_kernel,
        out_shape=(*(jax.ShapeDtypeStruct(field, F32) for _ in range(3)), jax.ShapeDtypeStruct((COLS,), F32)),
        in_specs=[vmem] * 6,
        out_specs=(hbm, hbm, hbm, vmem),
        scratch_shapes=[pltpu.VMEM(field, F32), pltpu.VMEM(field, F32), dma((2 * COLS + 1,))],
        compiler_params=pltpu.CompilerParams(vmem_limit_bytes=8 << 20),
        name="take_step",
    )(step, rr, solution, residual, new_dir, image)
    return new_solution, new_residual, out_dir, new_product


def solution(mesh):
    field = P("band", "grid", None, None)
    return jax.shard_map(
        functools.partial(on_device, mesh.shape["grid"]),
        mesh=mesh,
        in_specs=(
            field,
            field,
            field,
            P("band"),
            field,
            P(),
            P("grid", None, None),
            P("band"),
            P("band"),
        ),
        out_specs=(field, field, field, P("band")),
        check_vma=False,
    )
```

```python
import functools

import jax
import jax.numpy as jnp
from jax import lax
from jax.experimental import pallas as pl
from jax.experimental.pallas import tpu as pltpu
from jax.sharding import PartitionSpec as P

MESH = pl.DeviceIdType.MESH
F32 = jnp.float32
BF16 = jnp.bfloat16

PB = 16
K0, K1, K2, K3 = (-49.0 / 18.0, 3.0 / 2.0, -3.0 / 20.0, 1.0 / 90.0)
SCALED = (135.0, -13.5, 1.0)
UNSCALE = -0.5 / 90.0

COLS = 8
BANDS = 8
XS = 8
NY = 32
NZ = 384
HALF = 16
HALO = 3
FACES = (pl.ds(0, HALO), pl.ds(XS - HALO, HALO))
PIECES = (pl.ds(0, 2), pl.ds(XS - 2, 2), pl.ds(2, 1), pl.ds(XS - 3, 1), pl.ds(HALO, XS - 2 * HALO))
TURNS = 4


def iota(shape, dim):
    return lax.broadcasted_iota(jnp.int32, shape, dim)


def coefficient(distance):
    gap = jnp.abs(distance)
    return jnp.where(
        gap == 1, SCALED[0], jnp.where(gap == 2, SCALED[1], jnp.where(gap == 3, SCALED[2], 0.0))
    )


def dot(left, right, dims=((1,), (0,)), precision=None):
    return lax.dot_general(
        left, right, (dims, ((), ())), precision=precision, preferred_element_type=F32
    )


def first_kernel(
    groups,
    res_hbm,
    dir_hbm,
    orb_hbm,
    pot_hbm,
    old_hbm,
    energy_hbm,
    column_hbm,
    panel_hbm,
    solution_hbm,
    new_dir,
    image,
    rr_out,
    step_out,
    residual_near,
    solution_near,
    start,
    direction,
    pot,
    wave,
    left,
    kron,
    kron_mask,
    kron_ones,
    sten,
    sten_z,
    halo_wave,
    halo_out,
    halo_start,
    halo_in,
    halo_dir,
    sums,
    curves,
    partial,
    old_ref,
    energy_ref,
    column_ref,
    panel_ref,
    local_sem,
    ring_send,
    ring_recv,
    sum_send,
    sum_recv,
    halo_send,
    halo_recv,
):
    g = lax.axis_index("grid")
    z = lax.axis_index("band")
    up, down = lax.rem(z + 1, 4), lax.rem(z + 3, 4)

    loads = [
        pltpu.make_async_copy(src, dst, local_sem.at[i])
        for i, (src, dst) in enumerate(
            (
                (column_hbm, column_ref),
                (energy_hbm, energy_ref),
                (pot_hbm, pot),
                (res_hbm, start),
                (orb_hbm, wave.at[0]),
                (dir_hbm, direction),
                (old_hbm, old_ref),
                (panel_hbm, panel_ref),
                (res_hbm, residual_near),
                (solution_hbm, solution_near),
            )
        )
    ]
    def far(i):
        steps = (i // 8, i // 2 % 4)
        return -sum(min(n, 4 - n) for n in steps)

    order = sorted(range(1, groups), key=far)

    barrier = pltpu.get_barrier_semaphore()
    for to in (up, down):
        pl.semaphore_signal(barrier, inc=1, device_id=(g, to), device_id_type=MESH)

    for k in order:
        pl.semaphore_signal(
            barrier, inc=1, device_id=(lax.rem(g + k, groups), z), device_id_type=MESH
        )
    pl.semaphore_wait(barrier, groups + 1)

    def ring(src, dst, i, to):
        return pltpu.make_async_remote_copy(
            src_ref=src,
            dst_ref=dst,
            send_sem=ring_send.at[i],
            recv_sem=ring_recv.at[i],
            device_id=(g, to),
            device_id_type=MESH,
        )

    sides = (lax.rem(g + groups - 1, groups), lax.rem(g + 1, groups))

    def halo(src, dst, i, face):
        return pltpu.make_async_remote_copy(
            src_ref=src,
            dst_ref=dst,
            send_sem=halo_send.at[i],
            recv_sem=halo_recv.at[i],
            device_id=(sides[face], z),
            device_id_type=MESH,
        )

    landing = (pl.ds(HALO, HALO), pl.ds(0, HALO))
    halos = []

    def send_faces(slot, bands, src=None):
        src = wave.at[slot] if src is None else src
        for face in range(2):
            send_face(slot, bands, face, src, FACES[face], landing[face])

    def send_face(slot, bands, face, src, planes, place):
        copy = halo(src.at[bands, planes], halo_wave.at[slot, bands, place], len(halos), face)
        copy.start()
        halos.append(copy)

    low, high = pl.ds(0, BANDS // 2), pl.ds(BANDS // 2, BANDS // 2)
    low_up = ring(orb_hbm.at[low], wave.at[1, low], 0, up)
    high_down = ring(orb_hbm.at[high], wave.at[3, high], 1, down)
    high_up = ring(orb_hbm.at[high], wave.at[1, high], 2, up)
    low_down = ring(orb_hbm.at[low], wave.at[3, low], 3, down)
    low_up.start()
    high_down.start()
    high_up.start()
    low_down.start()
    for load in loads[:5]:
        load.start()
    rows, cols = iota((256, 448), 0), iota((256, 448), 1)
    plane = cols // NY
    there = jnp.where(plane < XS, plane, jnp.where(plane < XS + HALO, plane - XS - HALO, plane - HALO))
    inside = jnp.where(plane < XS, 1, jnp.where(plane < XS + HALO, g, groups - 1 - g)) > 0
    dx, dy = rows // NY - there, rows % NY - cols % NY
    weight = jnp.where(dy == 0, coefficient(dx), jnp.where(dx == 0, coefficient(dy), 0.0))
    sten[...] = jnp.where(inside, weight, 0.0).astype(BF16)
    sten_z[...] = coefficient(iota((NZ, NZ), 0) - iota((NZ, NZ), 1)).astype(BF16)

    def shift_of(c):
        return energy_ref[column_ref[c] // 3]

    for load in loads[:4]:
        load.wait()

    def start_column(c, _):
        e = shift_of(c)

        def start_plane(x, total):
            r = start[c, x]
            s = r / (pot[x] - e - 1.5 * K0)
            start[c, x] = s
            for h in range(2):
                part = slice(h * HALF, (h + 1) * HALF)
                left[x, h, 0, c] = s[part].astype(BF16)
                left[x, h, 1, c] = r[part].astype(BF16)
            return total + jnp.sum((r * s).reshape(4, 8, NZ), axis=0)

        total = lax.fori_loop(0, XS, start_plane, jnp.zeros((8, NZ), F32))
        partial[c] = total[:, :128] + total[:, 128:256] + total[:, 256:]
        return 0

    for load in loads[5:]:
        load.start()
    lax.fori_loop(0, COLS, start_column, 0)
    send_faces(0, pl.ds(0, BANDS), orb_hbm)
    for face in range(2):
        copy = halo(start.at[:, FACES[face]], halo_start.at[:, landing[face]], len(halos), face)
        copy.start()
        halos.append(copy)
    loads[5].wait()

    def fill(c, _):
        for face in range(2):
            halo_out[face, c] = direction[c, FACES[face]].astype(BF16)
        return 0

    lax.fori_loop(0, COLS, fill, 0)
    for face in range(2):
        copy = halo(halo_out.at[face], halo_in.at[:, landing[face]], len(halos), face)
        copy.start()
        halos.append(copy)

    def correlate(slot, first, planes):
        def body(x, total):
            for h in range(2):
                total = total + dot(
                    left[x, h].reshape(256, NZ),
                    wave[slot, :, x, pl.ds(h * HALF, HALF), :].reshape(128, NZ),
                    ((1,), (1,)),
                )
            return total

        return lax.fori_loop(
            first, first + planes, body, jnp.zeros((256, 128), F32), unroll=planes <= HALO
        )

    lane = iota((8, 128), 1)
    own = jnp.sum(jnp.sum(partial[...], axis=1), axis=1, keepdims=True)
    same = iota((256, 128), 0) % HALF == iota((256, 128), 1) % HALF

    def fold(block, slot):
        rows = jnp.sum(jnp.where(same, block, 0.0).reshape(16, HALF, 128), axis=1)
        high = rows.astype(BF16).astype(F32)
        middle = (rows - high).astype(BF16).astype(F32)
        terms = jnp.concatenate([high, middle, rows - high - middle], axis=0).astype(BF16)
        pick = iota((128, 128), 0) // HALF + slot * BANDS
        ones = jnp.where(pick == iota((128, 128), 1), 1.0, 0.0).astype(BF16)
        parts = dot(terms, ones)
        parts = parts[:16] + parts[16:32] + parts[32:]
        return parts[:8] + pltpu.roll(parts[8:], 32, 1)

    loads[4].wait()
    mine = fold(correlate(0, 0, XS), 0)

    forwards = []
    low_up.wait_recv()
    for q, part in enumerate(PIECES):
        copy = ring(wave.at[1, low, part], wave.at[2, low, part], 4 + 2 * q, up)
        copy.start()
        forwards.append(copy)
    high_down.wait_recv()
    for q, part in enumerate(PIECES):
        copy = ring(wave.at[3, high, part], wave.at[2, high, part], 5 + 2 * q, down)
        copy.start()
        forwards.append(copy)
    send_faces(1, low)
    send_faces(3, high)
    high_up.wait_recv()
    send_faces(1, high)
    low_down.wait_recv()
    send_faces(3, low)
    mine = mine + fold(correlate(1, 0, XS), 1)
    mine = mine + fold(correlate(3, 0, XS), 3)
    mine = mine + jnp.where(lane == 64, own, 0.0)
    for q, part in enumerate(PIECES):
        forwards[q].wait_recv()
        forwards[len(PIECES) + q].wait_recv()
        if q < TURNS:
            place = pl.ds(part.start + (HALO if q % 2 == 0 else HALO - XS), part.size)
            send_face(2, pl.ds(0, BANDS), q % 2, wave.at[2], part, place)
        term = correlate(2, part.start, part.size)
        last = term if q == 0 else last + term
    mine = mine + fold(last, 2)

    def send_over_grid(table, value, k):
        rows = pl.ds(0, value.shape[0])
        table[g, rows] = value

        for i in order:
            pltpu.make_async_remote_copy(
                src_ref=table.at[g, rows],
                dst_ref=table.at[g, rows],
                send_sem=sum_send.at[k],
                recv_sem=sum_recv.at[k],
                device_id=(lax.rem(g + i, groups), z),
                device_id_type=MESH,
            ).start()
    def sum_over_grid(table, k, count):
        others = table.at[pl.ds(0, groups - 1), pl.ds(0, count)]
        pltpu.make_async_copy(others, others, sum_recv.at[k]).wait()
        return jnp.sum(table[:, :count], axis=0)

    send_over_grid(sums, mine, 0)

    for load in loads[6:]:
        load.wait()
    owner = lax.rem(z + jnp.where(lane < 8, 0, jnp.where(lane < 16, 3, jnp.where(lane < 24, 2, 1))), 4)
    column = iota((8, 128), 0)
    panel = jnp.zeros((8, 128), jnp.int32)
    old = jnp.zeros((8, 128), F32)
    for c in range(COLS):
        panel = jnp.where(column == c, panel_ref[c], panel)
        old = jnp.where(column == c, old_ref[c], old)
    mask = jnp.where(iota((256, 512), 0) % HALF == iota((256, 512), 1) % HALF, 1.0, 0.0)
    kron_mask[...] = mask.astype(BF16)
    widen = jnp.where(iota((128, 512), 1) // HALF == iota((128, 512), 0), 1.0, 0.0)
    kron_ones[...] = widen.astype(BF16)
    member = jnp.logical_and(lane < 32, owner * BANDS // PB == panel)
    for copy in halos:
        copy.wait_recv()
    total = sum_over_grid(sums, 0, 8)

    cells = float(groups * XS * NY * NZ)
    chosen = jnp.where(member, total, 0.0) / cells
    overlap = pltpu.roll(total, 96, 1)
    rr = jnp.sum(
        jnp.where(lane == 64, total, 0.0) - chosen * overlap, axis=1, keepdims=True
    )
    rr = jnp.broadcast_to(rr, (8, 128))
    rr_out[...] = rr
    beta = rr / old

    top = chosen.astype(BF16)
    rest = (chosen - top.astype(F32)).astype(BF16)
    pair = jnp.concatenate([top.astype(F32), rest.astype(F32)], axis=0).astype(BF16)
    spread = dot(pair, kron_ones[...])
    spread = jnp.broadcast_to(spread[:, None, :], (16, HALF, 512)).reshape(256, 512)
    kron[...] = spread.astype(BF16) * kron_mask[...]

    def removed(source, x):
        plane = [
            source[:, :, x, h * HALF : (h + 1) * HALF, :].reshape(512, NZ) for h in range(2)
        ]
        both = dot(kron[...], jnp.concatenate(plane, axis=1))
        both = both[:128] + both[128:]
        return lambda c, h: both[c * HALF : (c + 1) * HALF, h * NZ : (h + 1) * NZ]

    for x in range(XS):
        gone = removed(wave, x)
        for c in range(COLS):
            for h in range(2):
                part = slice(h * HALF, (h + 1) * HALF)
                new_dir[c, x, part] = (
                    start[c, x, part] - gone(c, h) + beta[c : c + 1, :1] * direction[c, x, part]
                )
    for x in range(2 * HALO):
        gone = removed(halo_wave, x)
        for c in range(COLS):
            for h in range(2):
                part = slice(h * HALF, (h + 1) * HALF)
                halo_dir[c, x, part] = (
                    halo_start[c, x, part]
                    - gone(c, h)
                    + beta[c : c + 1, :1] * halo_in[c, x, part].astype(F32)
                ).astype(BF16)

    for first in range(0, COLS, 2):
        pair = [new_dir[c].reshape(256, NZ) for c in (first, first + 1)]
        tops = [value.astype(BF16) for value in pair]
        around = [
            jnp.concatenate([top, halo_dir[first + i].reshape(192, NZ)], axis=0)
            for i, top in enumerate(tops)
        ]
        across = dot(sten[...], jnp.concatenate(around, axis=1))
        for i, (value, top) in enumerate(zip(pair, tops)):
            c = first + i
            along = [
                dot(top, sten_z[:, 0:256]),
                dot(top[:, 128:384], sten_z[128:384, 256:384]),
            ]
            beside = across[:, i * NZ : (i + 1) * NZ] + jnp.concatenate(along, axis=1)
            local = pot[...].reshape(256, NZ) - (shift_of(c) + 1.5 * K0)
            full = UNSCALE * beside + local * value
            image[c] = full.reshape(XS, NY, NZ)
            total = jnp.sum((full * value).reshape(32, 8, NZ), axis=0)
            partial[c] = total[:, :128] + total[:, 128:256] + total[:, 256:]
    diagonal = iota((8, 128), 0) == lane
    curved = jnp.sum(jnp.sum(partial[...], axis=1), axis=1, keepdims=True)
    send_over_grid(curves, jnp.sum(jnp.where(diagonal, curved, 0.0), axis=0, keepdims=True), 1)

    def drain(table, k, count):
        others = table.at[pl.ds(0, groups - 1), pl.ds(0, count)]
        pltpu.make_async_copy(others, others, sum_send.at[k]).wait()

    drain(sums, 0, 8)
    for copy in (low_up, high_down, high_up, low_down, *forwards, *halos):
        copy.wait_send()
    drain(curves, 1, 1)
    curvature = jnp.where(diagonal, sum_over_grid(curves, 1, 1), 0.0)
    curvature = jnp.sum(curvature, axis=1, keepdims=True)
    step_out[...] = rr / curvature


def last_kernel(
    step, rr, solution_in, residual_in, new_dir, image, solution_hbm, residual_hbm, dir_hbm, rr_out, solution_new, residual_new, sems
):
    copies = [pltpu.make_async_copy(new_dir, dir_hbm, sems.at[2 * COLS])]
    copies[0].start()
    lane, row = iota((8, 128), 1), iota((8, 128), 0)
    rr_out[...] = jnp.sum(jnp.where(lane == row, rr[...], 0.0), axis=0)[:COLS]
    for c in range(COLS):
        alpha = step[c : c + 1, :1]
        solution_new[c] = solution_in[c] + alpha * new_dir[c]
        residual_new[c] = residual_in[c] - alpha * image[c]
        for i, (src, dst) in enumerate(((solution_new, solution_hbm), (residual_new, residual_hbm))):
            copy = pltpu.make_async_copy(src.at[c], dst.at[c], sems.at[2 * c + i])
            copy.start()
            copies.append(copy)
    for copy in copies:
        copy.wait()


def on_device(groups, residual, direction, solution, old_product, orbitals, energies, potential, column_index, panel_index):
    field = (COLS, XS, NY, NZ)
    hbm = pl.BlockSpec(memory_space=pltpu.HBM)
    vmem = pl.BlockSpec(memory_space=pltpu.VMEM)
    dma = pltpu.SemaphoreType.DMA
    new_dir, image, rr, step, residual, solution = pl.pallas_call(
        functools.partial(first_kernel, groups),
        out_shape=(
            jax.ShapeDtypeStruct(field, F32),
            jax.ShapeDtypeStruct(field, F32),
            jax.ShapeDtypeStruct((8, 128), F32),
            jax.ShapeDtypeStruct((8, 128), F32),
            jax.ShapeDtypeStruct(field, F32),
            jax.ShapeDtypeStruct(field, F32),
        ),
        in_specs=[hbm] * 9,
        out_specs=(vmem,) * 6,
        scratch_shapes=[
            pltpu.VMEM(field, F32),
            pltpu.VMEM(field, F32),
            pltpu.VMEM((XS, NY, NZ), F32),
            pltpu.VMEM((4, BANDS, XS, NY, NZ), BF16),
            pltpu.VMEM((XS, 2, 2, COLS, HALF, NZ), BF16),
            pltpu.VMEM((256, 512), BF16),
            pltpu.VMEM((256, 512), BF16),
            pltpu.VMEM((128, 512), BF16),
            pltpu.VMEM((256, 448), BF16),
            pltpu.VMEM((NZ, NZ), BF16),
            pltpu.VMEM((4, BANDS, 2 * HALO, NY, NZ), BF16),
            pltpu.VMEM((2, COLS, HALO, NY, NZ), BF16),
            pltpu.VMEM((COLS, 2 * HALO, NY, NZ), F32),
            pltpu.VMEM((COLS, 2 * HALO, NY, NZ), BF16),
            pltpu.VMEM((COLS, 2 * HALO, NY, NZ), BF16),
            pltpu.VMEM((groups, 8, 128), F32),
            pltpu.VMEM((groups, 8, 128), F32),
            pltpu.VMEM((COLS, 8, 128), F32),
            pltpu.SMEM((COLS,), F32),
            pltpu.SMEM((32,), F32),
            pltpu.SMEM((COLS,), jnp.int32),
            pltpu.SMEM((COLS,), jnp.int32),
            dma((10,)),
            dma((4 + 2 * len(PIECES),)),
            dma((4 + 2 * len(PIECES),)),
            dma((2,)),
            dma((2,)),
            dma((14 + TURNS,)),
            dma((14 + TURNS,)),
        ],
        compiler_params=pltpu.CompilerParams(
            collective_id=0, has_side_effects=True, vmem_limit_bytes=38 << 20
        ),
        name="project_and_apply",
    )(
        *(
            pltpu.with_memory_space_constraint(operand, pltpu.HBM)
            for operand in (
                residual,
                direction,
                orbitals,
                potential,
                old_product,
                energies,
                column_index,
                panel_index,
                solution,
            )
        )
    )

    new_solution, new_residual, out_dir, new_product = pl.pallas_call(
        last_kernel,
        out_shape=(*(jax.ShapeDtypeStruct(field, F32) for _ in range(3)), jax.ShapeDtypeStruct((COLS,), F32)),
        in_specs=[vmem] * 6,
        out_specs=(hbm, hbm, hbm, vmem),
        scratch_shapes=[pltpu.VMEM(field, F32), pltpu.VMEM(field, F32), dma((2 * COLS + 1,))],
        compiler_params=pltpu.CompilerParams(vmem_limit_bytes=8 << 20),
        name="take_step",
    )(step, rr, solution, residual, new_dir, image)
    return new_solution, new_residual, out_dir, new_product


def solution(mesh):
    field = P("band", "grid", None, None)
    return jax.shard_map(
        functools.partial(on_device, mesh.shape["grid"]),
        mesh=mesh,
        in_specs=(
            field,
            field,
            field,
            P("band"),
            field,
            P(),
            P("grid", None, None),
            P("band"),
            P("band"),
        ),
        out_specs=(field, field, field, P("band")),
        check_vma=False,
    )
```
